32 devices in a mesh: pb: 4 (over z), pa: 8 (over y, x, core).
Axes of the slice: x: 2, y: 2, z: 4, core: 2. Of those that a mesh axis runs over, the one named last changes fastest.
Arguments:
- queries: float32 [4096, 768], P(('pb', 'pa')), may hold values from -5 to 5
- passages: float32 [4096, 768], P(('pb', 'pa')), may hold values from -5 to 5
- hard_ids: int32 [4096, 32], P(('pb', 'pa')), may hold values from 0 to 4095, as said below
- list_lengths: int32 [4096], P(('pb', 'pa')), may hold values from 1 to 32, 98304 in all
Outputs:
- loss: float32 [], replicated
- grad_queries: float32 [4096, 768], P(('pb', 'pa'))
- grad_passages: float32 [4096, 768], P(('pb', 'pa'))
The draws below stay inside these ranges and needn't reach their ends.
Inputs may be any that keep to these rules, and one draw needn't show every extreme that they name: `hard_ids`: cut the rows into aligned blocks of 128 (the rows of one device) and the passage ids into blocks of 128 consecutive ids: the 32 listed ids of one row block, live or not, fall at most 160 times into any one id block; in every draw some id block receives exactly 160 ids from every row block.
All inputs are finite; a program needn't handle non-finite values. No bound on the sum of `list_lengths` on one device may be relied on, other than what follows from the above.
Results may differ from the reference program's by a relative error of at most 0.0014.
The reference program's roundings to bfloat16 on the way count: a program that leaves them out, or rounds other values in their place, can miss the bound.
Values may be sent and summed in bfloat16 or wider, within the bound.
No kernel may reach another device: no remote copies, remote signals or barrier semaphores. Data moves between devices by JAX's collectives and lax.ppermute only.
A program may use at most 128 MiB of HBM per device.

```python
import math
import jax
import jax.numpy as jnp
import numpy as np
from jax import lax

D = 768
ROW_DEV = 128
H = 32
N = 4096
CAP = 160


def hard_layout(key):
    owner_total = N // ROW_DEV
    pair_count = ROW_DEV * H
    slot_total = owner_total * CAP
    base_key = jax.random.fold_in(key, 101)
    special = jax.random.randint(jax.random.fold_in(base_key, 1), (), 0, owner_total)
    block_keys = jax.random.split(jax.random.fold_in(base_key, 2), owner_total)
    slot_owner = jnp.arange(slot_total, dtype=jnp.int32) // CAP

    def one_block(block_key):
        first_key, second_key, third_key, fourth_key = jax.random.split(block_key, 4)
        extra = jax.random.randint(first_key, (), 0, owner_total)
        ranking = jax.random.permutation(second_key, slot_total).astype(jnp.int32)
        forced = (slot_owner == special) | (slot_owner == extra)
        ordering = jnp.where(forced, ranking - slot_total, ranking)
        chosen = slot_owner[jnp.argsort(ordering, stable=True)[:pair_count]]
        shuffled = jax.random.permutation(third_key, chosen)
        within = jax.random.randint(fourth_key, (pair_count,), 0, ROW_DEV)
        return (shuffled * ROW_DEV + within).reshape(ROW_DEV, H)
    return jax.vmap(one_block)(block_keys).reshape(N, H).astype(jnp.int32)


def embeddings(key):
    spread = D ** (-0.25) * 1.2
    low_log = math.log(0.55)
    high_log = math.log(1.8)
    noise_query = jax.random.normal(jax.random.fold_in(key, 201), (N, D), jnp.float32)
    noise_passage = jax.random.normal(jax.random.fold_in(key, 202), (N, D), jnp.float32)
    scale_query = jnp.exp(jax.random.uniform(jax.random.fold_in(key, 204), (N, 1), jnp.float32, low_log, high_log))
    scale_passage = jnp.exp(jax.random.uniform(jax.random.fold_in(key, 205), (N, 1), jnp.float32, low_log, high_log))
    passages = spread * scale_passage * noise_passage
    id_table = hard_layout(key)
    group_rows = math.gcd(N, 256)

    def neighbour_sum(id_part):
        return passages[id_part].sum(1)
    summed = lax.map(neighbour_sum, id_table.reshape(N // group_rows, group_rows, H)).reshape(N, D)
    queries = spread * scale_query * noise_query + 4.0 / H * summed
    return (jnp.clip(queries, -5.0, 5.0), jnp.clip(passages, -5.0, 5.0))


def draw_queries(key, part):
    return embeddings(key)[0].astype(jnp.float32)


def draw_passages(key, part):
    return embeddings(key)[1].astype(jnp.float32)


def draw_hard_ids(key, part):
    return hard_layout(key)


def profile(count, total, most, skew):
    portions = [(1 << 20) // math.isqrt(rank ** skew) + 1 for rank in range(2, count + 1)]
    surplus, counts = total - most - (count - 1), [1] * (count - 1)
    while surplus > 0:
        free = [i for i in range(count - 1) if counts[i] < most]
        mass, left = sum([portions[i] for i in free]), surplus
        for i in free:
            more = min(most - counts[i], max(1, left * portions[i] // mass), surplus)
            counts[i] = counts[i] + more
            surplus = surplus - more
    return np.array([most] + counts)


def ragged(key, number_of, total, reach, slope):
    if number_of == 2:
        one = jax.random.randint(key, (), max(1, total - reach), min(reach, total - 1) + 1)
        return jnp.stack([one, total - one])
    sizes = jnp.asarray(profile(number_of, total, reach, slope), jnp.int32)
    couples = (number_of - 1) // 2
    giver, receiver = sizes[1:1 + 2 * couples:2], sizes[2:2 + 2 * couples:2]
    slack = jnp.minimum(giver - 1, reach - receiver)
    shifted = jax.random.randint(jax.random.fold_in(key, 1), (couples,), 0, 1 << 20) % (slack + 1)
    sizes = sizes.at[1:1 + 2 * couples:2].set(giver - shifted).at[2:2 + 2 * couples:2].set(receiver + shifted)
    return sizes[jax.random.permutation(jax.random.fold_in(key, 2), number_of)]


def setup_inputs(seed: int = 0) -> dict:
    keys = jax.random.split(jax.random.key(seed), 5)
    queries = draw_queries(jax.random.fold_in(keys[4], 71), 0)
    passages = draw_passages(jax.random.fold_in(keys[4], 71), 0)
    hard_ids = draw_hard_ids(jax.random.fold_in(keys[4], 71), 0)
    list_lengths = ragged(keys[3], N, 3 * N * H // 4, H, 1).astype(jnp.int32)
    return dict(queries=queries, passages=passages, hard_ids=hard_ids, list_lengths=list_lengths)


def tile_scores(left_rows, right_rows):
    return lax.dot_general(left_rows, right_rows, (((1,), (1,)), ((), ())), preferred_element_type=jnp.float32)


def reference(queries, passages, hard_ids, list_lengths):
    query_bf = queries.astype(jnp.bfloat16)
    passage_bf = passages.astype(jnp.bfloat16)
    block_rows = math.gcd(N, 1024)
    block_count = N // block_rows
    live_mask = jnp.arange(H, dtype=jnp.int32)[None, :] < list_lengths[:, None]
    query_blocks = query_bf.reshape(block_count, block_rows, D)
    passage_blocks = passage_bf.reshape(block_count, block_rows, D)
    id_blocks = hard_ids.reshape(block_count, block_rows, H)
    live_blocks = live_mask.reshape(block_count, block_rows, H)

    def first_sweep(carried, inputs):
        col_top, col_total = carried
        query_part, id_part, live_part = inputs
        scores = tile_scores(query_part, passage_bf)
        neg_rows = passage_bf[id_part]
        hard_score = jnp.einsum("rd,rhd->rh", query_part.astype(jnp.float32), neg_rows.astype(jnp.float32))
        masked = jnp.where(live_part, hard_score, -jnp.inf)
        row_top = jnp.maximum(scores.max(1), masked.max(1))
        row_total = jnp.exp(scores - row_top[:, None]).sum(1) + jnp.exp(masked - row_top[:, None]).sum(1)
        row_level = row_top + jnp.log(row_total)
        new_top = jnp.maximum(col_top, scores.max(0))
        col_total = col_total * jnp.exp(col_top - new_top) + jnp.exp(scores - new_top[None, :]).sum(0)
        return (new_top, col_total), (row_level, masked)

    start_state = (jnp.full((N,), -jnp.inf, jnp.float32), jnp.zeros((N,), jnp.float32))
    (col_top, col_total), (row_levels, masked_all) = lax.scan(first_sweep, start_state, (query_blocks, id_blocks, live_blocks))
    column_lse = col_top + jnp.log(col_total)
    row_lse = row_levels.reshape(N)
    diagonal = jnp.einsum("rd,rd->r", query_bf.astype(jnp.float32), passage_bf.astype(jnp.float32))
    loss = (jnp.sum(row_lse - diagonal) + jnp.sum(column_lse - diagonal)) / (2.0 * N)

    def second_sweep(passage_acc, inputs):
        query_part, passage_part, id_part, masked, row_level = inputs
        scores = tile_scores(query_part, passage_bf)
        weights = (jnp.exp(scores - row_level[:, None]) + jnp.exp(scores - column_lse[None, :])).astype(jnp.bfloat16)
        query_term = jnp.dot(weights, passage_bf, preferred_element_type=jnp.float32)
        passage_acc = passage_acc + lax.dot_general(weights, query_part, (((0,), (0,)), ((), ())), preferred_element_type=jnp.float32)
        hard_weight = jnp.exp(masked - row_level[:, None]).astype(jnp.bfloat16)
        neg_rows = passage_bf[id_part]
        hard_query = jnp.einsum("rh,rhd->rd", hard_weight.astype(jnp.float32), neg_rows.astype(jnp.float32))
        contribution = hard_weight.astype(jnp.float32)[:, :, None] * query_part.astype(jnp.float32)[:, None, :]
        passage_acc = passage_acc.at[id_part.reshape(-1)].add(contribution.reshape(-1, D))
        grad_rows = 0.5 * (query_term + hard_query - 2.0 * passage_part.astype(jnp.float32))
        return passage_acc, grad_rows

    passage_acc, grad_blocks = lax.scan(
        second_sweep,
        jnp.zeros((N, D), jnp.float32),
        (query_blocks, passage_blocks, id_blocks, masked_all, row_levels),
    )
    grad_queries = grad_blocks.reshape(N, D)
    grad_passages = 0.5 * (passage_acc - 2.0 * query_bf.astype(jnp.float32))
    return (loss, grad_queries, grad_passages)
```

```python
import jax
import jax.numpy as jnp
from jax import lax
from jax.experimental import pallas as pl
from jax.experimental.pallas import tpu as pltpu
from jax.sharding import PartitionSpec as P

F32 = jnp.float32
BF16 = jnp.bfloat16
VMEM_LIMIT = 56 * 1024 * 1024
F16_TOP = 30000.0


def exchange(value, axis, turn):
    size = lax.axis_size(axis)
    return lax.ppermute(value, axis, [(i, i ^ turn) for i in range(size)])


def call(kernel, out_shape, scratch_shapes, cost, *operands, scalars=0):
    flops, moved = cost
    spaces = [pl.BlockSpec(memory_space=pltpu.SMEM)] * scalars
    spaces += [pl.BlockSpec(memory_space=pltpu.VMEM)] * (len(operands) - scalars)
    return pl.pallas_call(
        kernel,
        out_shape=out_shape,
        in_specs=spaces,
        out_specs=jax.tree.map(lambda _: pl.BlockSpec(memory_space=pltpu.VMEM), out_shape),
        scratch_shapes=scratch_shapes,
        compiler_params=pltpu.CompilerParams(vmem_limit_bytes=VMEM_LIMIT),
        cost_estimate=pl.CostEstimate(flops=flops, bytes_accessed=moved, transcendentals=0),
    )(*operands)


def count_listed(keys, row_slots, col_slots, rows, row_axis_size, place):
    listed = keys.shape[1]

    def kernel(place_ref, keys_ref, out_ref):
        down, across = place_ref[0], place_ref[1]
        steps = lax.broadcasted_iota(jnp.int32, (rows, rows), 0)

        def one_tile(index, carry):
            k, j = index // col_slots, index % col_slots
            base = ((down ^ j) * row_axis_size + across) * rows
            local = keys_ref[across ^ k] - base
            total = jnp.zeros((rows, rows), jnp.int32)
            for h in range(listed):
                total = total + jnp.where(local[h : h + 1, :] == steps, 1, 0)
            out_ref[
                pl.ds(pl.multiple_of(j * rows, rows), rows),
                pl.ds(pl.multiple_of(k * rows, rows), rows),
            ] = total.astype(F32).astype(BF16)
            return carry

        lax.fori_loop(0, row_slots * col_slots, one_tile, 0)

    tall, wide = row_slots * rows, col_slots * rows
    return call(
        kernel,
        jax.ShapeDtypeStruct((wide, tall), BF16),
        [],
        (tall * wide * listed * 3, tall * wide * 2),
        place,
        keys,
        scalars=1,
    )


def score_sweep(query_slots, passage_slots, counts):
    row_slots, col_slots = len(query_slots), len(passage_slots)
    rows, width = query_slots[0].shape
    tall, wide = row_slots * rows, col_slots * rows
    lanes = 2 * rows

    def kernel(*refs):
        q_refs, refs = refs[:row_slots], refs[row_slots:]
        p_refs, refs = refs[:col_slots], refs[col_slots:]
        c_ref, s_ref, row_ref, col_ref, q_all, p_all, top_acc, sum_acc = refs
        query_most = jnp.zeros((1, 1), F32)
        passage_most = jnp.zeros((1, 1), F32)
        for k in range(row_slots):
            part = q_refs[k][...]
            q_all[k * rows : (k + 1) * rows, :] = part
            most = jnp.max(jnp.abs(part.astype(F32)), axis=0, keepdims=True)
            query_most = jnp.maximum(query_most, jnp.max(most, axis=1, keepdims=True))
        for j in range(col_slots):
            part = p_refs[j][...]
            p_all[j * rows : (j + 1) * rows, :] = part
            most = jnp.max(jnp.abs(part.astype(F32)), axis=0, keepdims=True)
            passage_most = jnp.maximum(passage_most, jnp.max(most, axis=1, keepdims=True))
        row_ref[...] = jnp.zeros_like(row_ref)
        col_ref[...] = jnp.zeros_like(col_ref)
        row_ref[2:3, :] = jnp.broadcast_to(passage_most, (1, tall))
        col_ref[2:3, :] = jnp.broadcast_to(query_most, (1, wide))
        top_acc[...] = jnp.full_like(top_acc, -jnp.inf)
        sum_acc[...] = jnp.zeros_like(sum_acc)

        def first(t, carry):
            spot = pl.ds(pl.multiple_of(t * lanes, lanes), lanes)
            s_ref[:, spot] = lax.dot_general(
                p_all[...], q_all[spot, :], (((1,), (1,)), ((), ())), preferred_element_type=F32
            )
            top = jnp.full((1, lanes), -jnp.inf, F32)
            for j in range(col_slots):
                part = s_ref[j * rows : (j + 1) * rows, spot]
                top = jnp.maximum(top, jnp.max(part, axis=0, keepdims=True))
                here = slice(j * rows, (j + 1) * rows)
                top_acc[here, :] = jnp.maximum(
                    top_acc[here, :], jnp.maximum(part[:, :rows], part[:, rows:])
                )
            total = jnp.zeros((1, lanes), F32)
            for j in range(col_slots):
                here = slice(j * rows, (j + 1) * rows)
                times = 1.0 + c_ref[here, spot].astype(F32)
                total = total + jnp.sum(
                    jnp.exp(s_ref[here, spot] - top) * times, axis=0, keepdims=True
                )
            row_ref[0:1, spot] = top
            row_ref[1:2, spot] = total
            return carry

        lax.fori_loop(0, tall // lanes, first, 0)
        for j in range(col_slots):
            here = slice(j * rows, (j + 1) * rows)
            acc = top_acc[here, :]
            col_ref[0:1, here] = jnp.max(acc.T, axis=0, keepdims=True)
            top_acc[here, :] = jnp.broadcast_to(
                jnp.max(acc, axis=1, keepdims=True), (rows, rows)
            )

        def second(t, carry):
            spot = pl.ds(pl.multiple_of(t * rows, rows), rows)
            for j in range(col_slots):
                here = slice(j * rows, (j + 1) * rows)
                sum_acc[here, :] += jnp.exp(s_ref[here, spot] - top_acc[here, :])
            return carry

        lax.fori_loop(0, row_slots, second, 0)
        for j in range(col_slots):
            here = slice(j * rows, (j + 1) * rows)
            col_ref[1:2, here] = jnp.sum(sum_acc[here, :].T, axis=0, keepdims=True)

    return call(
        kernel,
        (
            jax.ShapeDtypeStruct((wide, tall), F32),
            jax.ShapeDtypeStruct((8, tall), F32),
            jax.ShapeDtypeStruct((8, wide), F32),
        ),
        [
            pltpu.VMEM((tall, width), BF16),
            pltpu.VMEM((wide, width), BF16),
            pltpu.VMEM((wide, rows), F32),
            pltpu.VMEM((wide, rows), F32),
        ],
        (2 * tall * wide * width, tall * wide * 6),
        *query_slots,
        *passage_slots,
        counts,
    )


def turned(value, turn, rows):
    slots = value.shape[1] // rows
    return jnp.concatenate(
        [value[:, (k ^ turn) * rows : ((k ^ turn) + 1) * rows] for k in range(slots)], axis=1
    )


def join(messages, turns, rows):
    values = [turned(m, t, rows) for m, t in zip(messages, turns)]
    top = values[0][0:1]
    most = values[0][2:3]
    for v in values[1:]:
        top = jnp.maximum(top, v[0:1])
        most = jnp.maximum(most, v[2:3])
    total = jnp.zeros_like(top)
    for v in values:
        total = total + v[1:2] * jnp.exp(v[0:1] - top)
    return top, total, most


def join_pair(own, other, rows):
    def kernel(own_ref, other_ref, out_ref):
        top, total, most = join([own_ref[...], other_ref[...]], [0, 1], rows)
        out_ref[...] = jnp.zeros_like(out_ref)
        out_ref[0:1, :] = top
        out_ref[1:2, :] = total
        out_ref[2:3, :] = most

    return call(
        kernel, jax.ShapeDtypeStruct(own.shape, F32), [], (own.size * 4, own.size * 8), own, other
    )


def weight_sweep(scores, counts, row_stats, row_turns, col_stats, col_turns, query_slots):
    rows, width = query_slots[0].shape
    wide, tall = scores.shape
    row_slots, col_slots = tall // rows, wide // rows
    n_row, n_col = len(row_stats), len(col_stats)

    def kernel(*refs):
        s_ref, c_ref, refs = refs[0], refs[1], refs[2:]
        r_refs, refs = refs[:n_row], refs[n_row:]
        k_refs, refs = refs[:n_col], refs[n_col:]
        q_refs, refs = refs[:row_slots], refs[row_slots:]
        hi_ref, lo_ref, own_ref = refs[:3]
        out_refs, refs = refs[3 : 2 + col_slots], refs[2 + col_slots :]
        info_ref, q_all, row_level, col_level = refs
        for k in range(row_slots):
            q_all[k * rows : (k + 1) * rows, :] = q_refs[k][...]
        top, total, passage_most = join([r[...] for r in r_refs], row_turns, rows)
        row_level[...] = top + jnp.log(total)
        top, total, query_most = join([r[...] for r in k_refs], col_turns, rows)
        columns = top + jnp.log(total)
        for j in range(col_slots):
            here = slice(j * rows, (j + 1) * rows)
            col_level[here, :] = jnp.broadcast_to(columns[:, here], (rows, rows)).T
        unit = (
            lax.broadcasted_iota(jnp.int32, (rows, rows), 0)
            == lax.broadcasted_iota(jnp.int32, (rows, rows), 1)
        ).astype(F32)
        for j in range(col_slots):
            here = slice(j * rows, (j + 1) * rows)

            def one(k, carry, here=here, j=j):
                spot = pl.ds(pl.multiple_of(k * rows, rows), rows)
                part = s_ref[here, spot]
                by_row = jnp.exp(part - row_level[:, spot])
                by_col = jnp.exp(part - col_level[here, :])
                pair = (by_row + by_col).astype(BF16).astype(F32)
                hard = by_row.astype(BF16).astype(F32)
                weight = pair + hard * c_ref[here, spot].astype(F32)
                if j == 0:
                    weight = weight - unit * jnp.where(k == 0, 2.0, 0.0)
                high = weight.astype(BF16)
                hi_ref[here, spot] = high
                lo_ref[here, spot] = (weight - high.astype(F32)).astype(BF16)
                return carry

            lax.fori_loop(0, row_slots, one, 0)
        query_scale = F16_TOP / jnp.maximum(query_most[:, :1] * (tall * 1.02 + 8.0), 1e-30)
        passage_scale = F16_TOP / jnp.maximum(
            passage_most[:, :1] * (2 * wide * 1.02 + 8.0), 1e-30
        )
        for j in range(col_slots):
            here = slice(j * rows, (j + 1) * rows)
            part = jnp.dot(hi_ref[here, :], q_all[...], preferred_element_type=F32)
            part = part + jnp.dot(lo_ref[here, :], q_all[...], preferred_element_type=F32)
            if j == 0:
                own_ref[...] = part
            else:
                out_refs[j - 1][...] = part * query_scale
        diagonal = jnp.sum(unit * s_ref[:rows, :rows], axis=0, keepdims=True)
        losses = row_level[:, :rows] + columns[:, :rows] - 2.0 * diagonal
        info_ref[...] = jnp.zeros_like(info_ref)
        info_ref[0:1, :] = jnp.broadcast_to(jnp.sum(losses, axis=1, keepdims=True), (1, rows))
        info_ref[1:2, :] = jnp.broadcast_to(query_scale, (1, rows))
        info_ref[2:3, :] = jnp.broadcast_to(passage_scale, (1, rows))

    block = jax.ShapeDtypeStruct((rows, width), F32)
    return call(
        kernel,
        (
            jax.ShapeDtypeStruct((wide, tall), BF16),
            jax.ShapeDtypeStruct((wide, tall), BF16),
            block,
            *[block] * (col_slots - 1),
            jax.ShapeDtypeStruct((8, rows), F32),
        ),
        [
            pltpu.VMEM((tall, width), BF16),
            pltpu.VMEM((1, tall), F32),
            pltpu.VMEM((wide, rows), F32),
        ],
        (4 * tall * wide * width, tall * wide * 10),
        scores,
        counts,
        *row_stats,
        *col_stats,
        *query_slots,
    )


def query_sweep(high, low, passage_slots):
    rows, width = passage_slots[0].shape
    wide, tall = high.shape
    row_slots, col_slots = tall // rows, wide // rows

    def kernel(*refs):
        hi_ref, lo_ref, refs = refs[0], refs[1], refs[2:]
        p_refs, refs = refs[:col_slots], refs[col_slots:]
        even_ref, odd_ref, p_all = refs
        for j in range(col_slots):
            p_all[j * rows : (j + 1) * rows, :] = p_refs[j][...]

        def one(m, carry):
            spot = pl.ds(pl.multiple_of(m * 2 * rows, 2 * rows), 2 * rows)
            dims = (((0,), (0,)), ((), ()))
            part = lax.dot_general(
                hi_ref[:, spot], p_all[...], dims, preferred_element_type=F32
            ) + lax.dot_general(lo_ref[:, spot], p_all[...], dims, preferred_element_type=F32)
            even_ref[m] = part[:rows]
            odd_ref[m] = part[rows:]
            return carry

        lax.fori_loop(0, row_slots // 2, one, 0)

    half = jax.ShapeDtypeStruct((row_slots // 2, rows, width), F32)
    return call(
        kernel,
        (half, half),
        [pltpu.VMEM((wide, width), BF16)],
        (4 * tall * wide * width, tall * wide * 4 + tall * width * 4),
        high,
        low,
        *passage_slots,
    )


def per_device(queries, passages, hard_ids, list_lengths):
    rows, width = queries.shape
    listed = hard_ids.shape[1]
    across = lax.axis_size("pa")
    down = lax.axis_size("pb")
    query_own = queries.astype(BF16)
    passage_own = passages.astype(BF16)

    live = jnp.arange(listed, dtype=jnp.int32)[None, :] < list_lengths[:, None]
    keys = jnp.where(live, hard_ids, -1).T
    keys = lax.all_gather(keys, "pa")
    place = jnp.stack([lax.axis_index("pb"), lax.axis_index("pa")]).astype(jnp.int32)
    counts = count_listed(keys, across, down, rows, across, place)

    passage_slots = [passage_own] + [exchange(passage_own, "pb", j) for j in range(1, down)]
    even = [query_own] + [exchange(query_own, "pa", k) for k in range(2, across, 2)]
    odd = [exchange(part, "pa", 1) for part in even]
    query_slots = [part for pair in zip(even, odd) for part in pair]

    scores, row_message, col_message = score_sweep(query_slots, passage_slots, counts)
    col_stats = [col_message] + [exchange(col_message, "pb", j) for j in range(1, down)]
    pair_message = join_pair(row_message, exchange(row_message, "pa", 1), rows)
    row_turns = list(range(0, across, 2))
    row_stats = [pair_message] + [exchange(pair_message, "pa", k) for k in row_turns[1:]]

    high, low, *blocks, info = weight_sweep(
        scores, counts, row_stats, row_turns, col_stats, list(range(down)), query_slots
    )
    passage_sum, sent = blocks[0], blocks[1:]
    arrived = [
        exchange(part.astype(jnp.float16), "pb", j) for j, part in enumerate(sent, start=1)
    ]
    even_sum, odd_sum = query_sweep(high, low, passage_slots)
    even_sum = even_sum + exchange(odd_sum, "pa", 1)
    passage_scale = info[2, 0]
    query_scale = info[1, 0]
    returned = [
        exchange((even_sum[k // 2] * passage_scale).astype(jnp.float16), "pa", k)
        for k in row_turns[1:]
    ]
    loss = info[0, 0]
    for axis, size in (("pa", across), ("pb", down)):
        turn = 1
        while turn < size:
            loss = loss + exchange(loss, axis, turn)
            turn *= 2
    loss = loss / (2.0 * rows * across * down)
    back = 0.5 / query_scale
    grad_passages = 0.5 * passage_sum + sum(part.astype(F32) for part in arrived) * back
    back = 0.5 / passage_scale
    grad_queries = 0.5 * even_sum[0] + sum(part.astype(F32) for part in returned) * back
    return (loss, grad_queries, grad_passages)


def solution(mesh):
    return jax.shard_map(
        per_device,
        mesh=mesh,
        in_specs=(
            P(("pb", "pa"), None),
            P(("pb", "pa"), None),
            P(("pb", "pa"), None),
            P(("pb", "pa")),
        ),
        out_specs=(P(), P(("pb", "pa"), None), P(("pb", "pa"), None)),
        check_vma=False,
    )
```

```python
import math

import jax
import jax.numpy as jnp
from jax import lax
from jax.experimental import pallas as pl
from jax.experimental.pallas import tpu as pltpu
from jax.sharding import PartitionSpec as P

F32 = jnp.float32
BF16 = jnp.bfloat16
VMEM_SPARE = 4 * 1024 * 1024
CODE_SPAN = 2.0**20
CODE_STEPS = 32000.0 / math.asinh(CODE_SPAN)
LOSS_UNIT = 1.0 / 4096.0
DIGIT = 2.0**15


def exchange(value, axis, turn):
    size = lax.axis_size(axis)
    return lax.ppermute(value, axis, [(i, i ^ turn) for i in range(size)])


def call(kernel, out_shape, scratch_shapes, *operands, spare=()):
    size = sum(x.size * x.dtype.itemsize for x in (*operands, *jax.tree.leaves(out_shape)))
    held = [x for x in scratch_shapes if hasattr(x, "memory_space") and x.memory_space == pltpu.VMEM]
    size += sum(math.prod(x.shape) * jnp.dtype(x.dtype).itemsize for x in held)
    spaces = [pl.BlockSpec(memory_space=pltpu.VMEM)] * len(operands)
    spaces += [pl.BlockSpec(memory_space=pl.ANY)] * len(spare)
    return pl.pallas_call(
        kernel,
        out_shape=out_shape,
        in_specs=spaces,
        out_specs=jax.tree.map(lambda _: pl.BlockSpec(memory_space=pltpu.VMEM), out_shape),
        scratch_shapes=scratch_shapes,
        compiler_params=pltpu.CompilerParams(vmem_limit_bytes=2 * size + VMEM_SPARE),
        cost_estimate=pl.CostEstimate(flops=1, bytes_accessed=1, transcendentals=0),
    )(*operands, *spare)


def first_messages(queries, passages, hard_ids, list_lengths):
    rows, width = queries.shape
    listed = hard_ids.shape[1]
    groups = listed // 16
    operands = (passages, hard_ids.T, list_lengths.reshape(1, rows), queries)

    def kernel(*refs):
        here, (p_out, q_out), refs = refs[:4], refs[4:6], refs[6:]
        p_ref, ids_ref, len_ref, q_ref = refs[:4]
        copies = [
            pltpu.make_async_copy(src, dst, refs[4].at[n])
            for n, (src, dst) in enumerate(zip(here, refs[:4]))
        ]
        for copy in copies:
            copy.start()
        for copy in copies:
            copy.wait()
        p_out[...] = p_ref[...].astype(BF16)
        q_out[:rows, :] = q_ref[...].astype(BF16)
        ids = ids_ref[...].astype(F32)
        live = lax.broadcasted_iota(jnp.int32, (listed, rows), 0) < len_ref[...]
        block = jnp.floor((ids + 0.5) * (1.0 / rows))
        inside = (ids - block * rows).astype(BF16)
        block = jnp.where(live, block, -1.0).astype(BF16)
        q_out[rows:, :] = jnp.zeros((16, width), BF16)
        for g in range(groups):
            part = slice(g * 16, (g + 1) * 16)
            q_out[rows:, g * rows : (g + 1) * rows] = block[part, :]
            q_out[rows:, (groups + g) * rows : (groups + g + 1) * rows] = inside[part, :]

    return call(
        kernel,
        (
            jax.ShapeDtypeStruct((rows, width), BF16),
            jax.ShapeDtypeStruct((rows + 16, width), BF16),
        ),
        [pltpu.VMEM(x.shape, x.dtype) for x in operands] + [pltpu.SemaphoreType.DMA((4,))],
        spare=operands,
    )


def tally(tail, rows, listed, col_slots, fields):
    groups = listed // 16
    down, across = lax.axis_index("pb"), lax.axis_index("pa")
    row_axis_size = lax.axis_size("pa")
    digits = [tail[:, g * rows : (g + 1) * rows].astype(F32) for g in range(2 * groups)]
    block = jnp.concatenate(digits[:groups], axis=0).astype(jnp.int32)
    inside = jnp.concatenate(digits[groups:], axis=0).astype(jnp.int32)
    steps = lax.broadcasted_iota(jnp.int32, (rows, rows), 0)
    for g in range(0, col_slots, 4):
        unit = jnp.zeros((listed, rows), jnp.int32)
        for j in range(g, min(g + 4, col_slots)):
            mine = (down ^ j) * row_axis_size + across
            unit = jnp.where(block == mine, 1 << (8 * (j - g)), unit)
        total = jnp.zeros((rows, rows), jnp.int32)
        for h in range(listed):
            total = total + jnp.where(inside[h : h + 1, :] == steps, unit[h : h + 1, :], 0)
        fields[g // 4] = total


def count_at(ref, m, j):
    return ((ref[m, j // 4] >> (8 * (j % 4))) & 255).astype(F32)


def gather_even(messages, col_slots, listed, after):
    slots = len(messages)
    tall, width = messages[0].shape
    rows = tall - 16

    def kernel(*refs):
        m_refs, (out_ref, count_ref) = refs[:slots], refs[-2:]
        for m in range(slots):
            out_ref[m] = m_refs[m][...]
            tally(m_refs[m][rows:, :], rows, listed, col_slots, count_ref.at[m])

    return call(
        kernel,
        (
            jax.ShapeDtypeStruct((slots, tall, width), BF16),
            jax.ShapeDtypeStruct((slots, -(-col_slots // 4), rows, rows), jnp.int32),
        ),
        [],
        *messages,
        spare=after,
    )


def count_odd(messages, col_slots, listed):
    slots, tall, width = messages.shape
    rows = tall - 16

    def kernel(m_ref, count_ref):
        for m in range(slots):
            tally(m_ref[m, rows:, :], rows, listed, col_slots, count_ref.at[m])

    return call(
        kernel,
        jax.ShapeDtypeStruct((slots, -(-col_slots // 4), rows, rows), jnp.int32),
        [],
        messages,
    )


def score_sweep(even, odd, passage_slots, even_counts, odd_counts):
    row_slots, col_slots = 2 * even.shape[0], len(passage_slots)
    rows, width = passage_slots[0].shape
    tall, wide = row_slots * rows, col_slots * rows

    def most_of(part):
        most = jnp.max(jnp.abs(part.astype(F32)), axis=0, keepdims=True)
        return jnp.max(most, axis=1, keepdims=True)

    def kernel(*refs):
        q_refs, refs = refs[:2], refs[2:]
        p_refs, refs = refs[:col_slots], refs[col_slots:]
        even_ref, odd_ref, s_ref, row_ref, col_ref, p_all, top_acc = refs
        row_ref[...] = jnp.zeros_like(row_ref)
        col_ref[...] = jnp.zeros_like(col_ref)
        passage_most = jnp.zeros((1, 1), F32)
        for j in range(col_slots):
            part = p_refs[j][...]
            p_all[j * rows : (j + 1) * rows, :] = part
            passage_most = jnp.maximum(passage_most, most_of(part))
        query_most = jnp.zeros((1, 1), F32)
        for m in range(row_slots // 2):
            both = jnp.concatenate([q[m, :rows, :] for q in q_refs], axis=0)
            query_most = jnp.maximum(query_most, most_of(both))
            spot = slice(2 * m * rows, 2 * (m + 1) * rows)
            s_ref[:, spot] = lax.dot_general(
                p_all[...], both, (((1,), (1,)), ((), ())), preferred_element_type=F32
            )
        row_ref[2:3, :] = jnp.broadcast_to(passage_most, (1, tall))
        unit = lax.broadcasted_iota(jnp.int32, (rows, rows), 0) == lax.broadcasted_iota(
            jnp.int32, (rows, rows), 1
        )
        pairs = jnp.sum(jnp.where(unit, s_ref[:rows, :rows], 0.0), axis=0, keepdims=True)
        row_ref[3:4, :] = jnp.broadcast_to(jnp.sum(pairs, axis=1, keepdims=True), (1, tall))
        col_ref[2:3, :] = jnp.broadcast_to(query_most, (1, wide))
        for k in range(row_slots):
            spot = slice(k * rows, (k + 1) * rows)
            c_ref = (even_ref, odd_ref)[k % 2]
            top = jnp.full((1, rows), -jnp.inf, F32)
            for j in range(col_slots):
                here = slice(j * rows, (j + 1) * rows)
                part = s_ref[here, spot]
                top = jnp.maximum(top, jnp.max(part, axis=0, keepdims=True))
                if k == 0:
                    top_acc[here, :] = part
                else:
                    top_acc[here, :] = jnp.maximum(top_acc[here, :], part)
            total = jnp.zeros((1, rows), F32)
            for j in range(col_slots):
                here = slice(j * rows, (j + 1) * rows)
                times = 1.0 + count_at(c_ref, k // 2, j)
                total = total + jnp.sum(
                    jnp.exp(s_ref[here, spot] - top) * times, axis=0, keepdims=True
                )
            row_ref[0:1, spot] = top
            row_ref[1:2, spot] = total
        for j in range(col_slots):
            here = slice(j * rows, (j + 1) * rows)
            acc = top_acc[here, :]
            col_ref[0:1, here] = jnp.max(acc.T, axis=0, keepdims=True)
            top = jnp.max(acc, axis=1, keepdims=True)
            total = jnp.zeros((rows, rows), F32)
            for k in range(row_slots):
                total = total + jnp.exp(s_ref[here, k * rows : (k + 1) * rows] - top)
            col_ref[1:2, here] = jnp.sum(total.T, axis=0, keepdims=True)

    return call(
        kernel,
        (
            jax.ShapeDtypeStruct((wide, tall), F32),
            jax.ShapeDtypeStruct((8, tall), F32),
            jax.ShapeDtypeStruct((8, wide), F32),
        ),
        [pltpu.VMEM((wide, width), BF16), pltpu.VMEM((wide, rows), F32)],
        even,
        odd,
        *passage_slots,
        even_counts,
        odd_counts,
    )


def turned(value, turn, rows):
    slots = value.shape[1] // rows
    return jnp.concatenate(
        [value[:, (k ^ turn) * rows : ((k ^ turn) + 1) * rows] for k in range(slots)], axis=1
    )


def tree(combine, values):
    while len(values) > 1:
        values = [combine(a, b) for a, b in zip(values[::2], values[1::2])]
    return values[0]


def join(own, other, turn, rows):
    def kernel(own_ref, other_ref, out_ref):
        one, two = own_ref[...], turned(other_ref[...], turn, rows)
        top = jnp.maximum(one[0:1], two[0:1])
        out_ref[0:1, :] = top
        out_ref[1:2, :] = one[1:2] * jnp.exp(one[0:1] - top) + two[1:2] * jnp.exp(two[0:1] - top)
        out_ref[2:3, :] = jnp.maximum(one[2:3], two[2:3])
        out_ref[3:, :] = one[3:] + two[3:]

    return call(kernel, jax.ShapeDtypeStruct(own.shape, F32), [], own, other)


def coded(value, inverse):
    size = jnp.abs(value) * (inverse * CODE_SPAN)
    steps = jnp.log(size + jnp.sqrt(size * size + 1.0)) * CODE_STEPS
    return jnp.round(jnp.where(value < 0.0, -steps, steps)).astype(jnp.int32).astype(jnp.int16)


def decoded(code, bound):
    grown = jnp.exp(code.astype(F32) * (1.0 / CODE_STEPS))
    return (grown - 1.0 / grown) * (bound * (0.5 / CODE_SPAN))


def write_term(ref, value):
    rows = ref.shape[0] - 16
    ref[rows:, :] = jnp.zeros((16, ref.shape[1]), jnp.int16)
    left = value[:, :1] * LOSS_UNIT
    for n in range(3):
        digit = jnp.round(left)
        left = (left - digit) * DIGIT
        ref[rows:, n * 128 : (n + 1) * 128] = (
            jnp.broadcast_to(digit, (16, 128)).astype(jnp.int32).astype(jnp.int16)
        )


def read_term(ref):
    rows = ref.shape[0] - 16
    one, two, three = [
        ref[rows:, n * 128 : (n + 1) * 128].astype(F32)[:1, :1] for n in range(3)
    ]
    return (one + (two + three * (1.0 / DIGIT)) * (1.0 / DIGIT)) * (1.0 / LOSS_UNIT)


def weight_sweep(scores, even_counts, odd_counts, row_stats, col_stats, even, odd):
    rows = even_counts.shape[2]
    width = even.shape[2]
    wide, tall = scores.shape
    row_slots, col_slots = tall // rows, wide // rows

    def kernel(*refs):
        (s_ref, even_ref, odd_ref), refs = refs[:3], refs[3:]
        (row_ref, col_ref), refs = refs[:2], refs[2:]
        q_refs, refs = refs[:2], refs[2:]
        (hi_ref, lo_ref), refs = refs[:2], refs[2:]
        out_refs, refs = refs[:col_slots], refs[col_slots:]
        info_ref, q_all, row_level, col_level = refs
        for k in range(row_slots):
            q_all[k * rows : (k + 1) * rows, :] = q_refs[k % 2][k // 2, :rows, :]
        row_level[...] = row_ref[0:1, :] + jnp.log(row_ref[1:2, :])
        columns = col_ref[0:1, :] + jnp.log(col_ref[1:2, :])
        query_most = col_ref[2:3, :]
        passage_most, pairs = row_ref[2:3, :], row_ref[3:4, :]
        for j in range(col_slots):
            here = slice(j * rows, (j + 1) * rows)
            col_level[here, :] = jnp.broadcast_to(columns[:, here], (rows, rows)).T
        unit = (
            lax.broadcasted_iota(jnp.int32, (rows, rows), 0)
            == lax.broadcasted_iota(jnp.int32, (rows, rows), 1)
        ).astype(F32)
        query_bound = jnp.maximum(query_most[:, :1] * (tall * 1.02 + 8.0), 1e-30)
        passage_bound = jnp.maximum(passage_most[:, :1] * (2 * wide * 1.02 + 8.0), 1e-30)
        inverse = 1.0 / query_bound
        for j in reversed(range(col_slots)):
            here = slice(j * rows, (j + 1) * rows)
            for k in range(row_slots):
                spot = slice(k * rows, (k + 1) * rows)
                c_ref = (even_ref, odd_ref)[k % 2]
                part = s_ref[here, spot]
                by_row = jnp.exp(part - row_level[:, spot])
                by_col = jnp.exp(part - col_level[here, :])
                pair = (by_row + by_col).astype(BF16).astype(F32)
                hard = by_row.astype(BF16).astype(F32)
                weight = pair + hard * count_at(c_ref, k // 2, j)
                if j == 0 and k == 0:
                    weight = weight - 2.0 * unit
                high = weight.astype(BF16)
                hi_ref[here, spot] = high
                lo_ref[here, spot] = (weight - high.astype(F32)).astype(BF16)
            part = jnp.dot(hi_ref[here, :], q_all[...], preferred_element_type=F32)
            part = part + jnp.dot(lo_ref[here, :], q_all[...], preferred_element_type=F32)
            if j % 2 == 0:
                out_refs[j][...] = part
            else:
                out_refs[j][:rows, :] = coded(part, inverse)

        def summed(level):
            parts = [
                jnp.sum(level[:, g * rows : (g + 1) * rows], axis=1, keepdims=True)
                for g in range(level.shape[1] // rows)
            ]
            return tree(jnp.add, parts)

        row_term = summed(row_level[...]) - 2.0 * pairs[:, :1]
        info_ref[...] = jnp.zeros_like(info_ref)
        for n, value in enumerate((row_term, summed(columns), query_bound, passage_bound)):
            info_ref[n : n + 1, :] = jnp.broadcast_to(value, (1, rows))
        for j in range(1, col_slots, 2):
            write_term(out_refs[j], row_term)

    return call(
        kernel,
        (
            jax.ShapeDtypeStruct((wide, tall), BF16),
            jax.ShapeDtypeStruct((wide, tall), BF16),
            *[
                jax.ShapeDtypeStruct((rows, width), F32),
                jax.ShapeDtypeStruct((rows + 16, width), jnp.int16),
            ]
            * (col_slots // 2),
            jax.ShapeDtypeStruct((8, rows), F32),
        ),
        [
            pltpu.VMEM((tall, width), BF16),
            pltpu.VMEM((1, tall), F32),
            pltpu.VMEM((wide, rows), F32),
        ],
        scores,
        even_counts,
        odd_counts,
        row_stats,
        col_stats,
        even,
        odd,
    )


def query_sweep(high, low, passage_slots, info):
    rows, width = passage_slots[0].shape
    wide, tall = high.shape
    row_slots, col_slots = tall // rows, wide // rows
    half = row_slots // 2 * rows

    def kernel(*refs):
        (hi_ref, lo_ref), refs = refs[:2], refs[2:]
        p_refs, refs = refs[:col_slots], refs[col_slots:]
        info_ref, even_ref, odd_ref, p_all = refs
        for j in range(col_slots):
            p_all[j * rows : (j + 1) * rows, :] = p_refs[j][...]
        for m in range(row_slots // 2):
            spot = slice(m * 2 * rows, (m + 1) * 2 * rows)
            dims = (((0,), (0,)), ((), ()))
            part = lax.dot_general(
                hi_ref[:, spot], p_all[...], dims, preferred_element_type=F32
            ) + lax.dot_general(lo_ref[:, spot], p_all[...], dims, preferred_element_type=F32)
            even_ref[m * rows : (m + 1) * rows, :] = part[:rows]
            odd_ref[m * rows : (m + 1) * rows, :] = part[rows:]
        odd_ref[half:, :] = jnp.zeros((8, width), F32)
        odd_ref[half : half + 8, :rows] = info_ref[...]

    return call(
        kernel,
        (
            jax.ShapeDtypeStruct((half, width), F32),
            jax.ShapeDtypeStruct((half + 8, width), F32),
        ),
        [pltpu.VMEM((wide, width), BF16)],
        high,
        low,
        *passage_slots,
        info,
    )


def middle(even, other, info, halves, relayed):
    rows = info.shape[1]
    half, width = even.shape
    slots = half // rows
    passed = len(relayed)

    def kernel(even_ref, other_ref, info_ref, *refs):
        half_refs, relay_refs, refs = refs[:passed], refs[passed : 2 * passed], refs[2 * passed :]
        own_ref, term_ref, refs = refs[0], refs[1], refs[2:]
        query_bound = info_ref[2:3, :1]
        inverse = 1.0 / query_bound
        row_term = info_ref[0:1, :1]
        if passed:
            for half_ref, relay_ref, out_ref in zip(half_refs, relay_refs, refs):
                total = half_ref[...] + decoded(relay_ref[:rows, :], query_bound)
                out_ref[:rows, :] = coded(total, inverse)
            row_term = row_term + read_term(relay_refs[0])
            for out_ref in refs[:passed]:
                write_term(out_ref, row_term)
        inverse = 1.0 / info_ref[3:4, :1]
        own_ref[...] = even_ref[:rows, :] + other_ref[:rows, :]
        col_term = info_ref[1:2, :1] + other_ref[half + 1 : half + 2, :1]
        for m in range(1, slots):
            here = slice(m * rows, (m + 1) * rows)
            out_ref = refs[passed + m - 1]
            out_ref[:rows, :] = coded(even_ref[here, :] + other_ref[here, :], inverse)
            write_term(out_ref, col_term)
        term_ref[...] = jnp.zeros_like(term_ref)
        term_ref[0:1, :] = jnp.broadcast_to(row_term, (1, rows))
        term_ref[1:2, :] = jnp.broadcast_to(col_term, (1, rows))

    return call(
        kernel,
        (
            jax.ShapeDtypeStruct((rows, width), F32),
            jax.ShapeDtypeStruct((8, rows), F32),
            *[jax.ShapeDtypeStruct((rows + 16, width), jnp.int16)] * (passed + slots - 1),
        ),
        [],
        even,
        other,
        info,
        *halves,
        *relayed,
    )


def finish(own, arrived, info, row):
    rows, width = own.shape

    def kernel(own_ref, info_ref, *refs):
        bound = info_ref[row : row + 1, :1]
        total = own_ref[...]
        for a in refs[:-1]:
            total = total + decoded(a[:rows, :], bound)
        refs[-1][...] = 0.5 * total

    return call(kernel, jax.ShapeDtypeStruct((rows, width), F32), [], own, info, *arrived)


def mean_loss(term, across, along, devices):
    rows = term.shape[1]

    def kernel(term_ref, *refs):
        sides = [term_ref[1:2, :1]] + [read_term(a) for a in refs[: len(across)]]
        lines = [term_ref[0:1, :1]] + [read_term(a) for a in refs[len(across) : -1]]
        loss = tree(jnp.add, sides) + tree(jnp.add, lines)
        refs[-1][...] = loss * (1.0 / (2.0 * rows * devices))

    return call(kernel, jax.ShapeDtypeStruct((1, 1), F32), [], term, *across, *along)


def per_device(queries, passages, hard_ids, list_lengths):
    rows, width = queries.shape
    listed = hard_ids.shape[1]
    across = lax.axis_size("pa")
    down = lax.axis_size("pb")
    passage_own, message = first_messages(queries, passages, hard_ids, list_lengths)
    far = [exchange(passage_own, "pb", j) for j in range(2, down, 2)]
    near = exchange(passage_own, "pb", 1)
    row_turns = list(range(0, across, 2))
    even = [message] + [exchange(message, "pa", k) for k in row_turns[1:]]
    even, even_counts = gather_even(even, down, listed, far + [near])
    passage_slots = [passage_own, near]
    for part in far:
        passage_slots += [part, exchange(part, "pb", 1)]
    odd = exchange(even, "pa", 1)
    odd_counts = count_odd(odd, down, listed)

    scores, row_stats, col_stats = score_sweep(
        even, odd, passage_slots, even_counts, odd_counts
    )
    turn = 1
    while turn < max(across, down):
        if turn < across:
            row_stats = join(row_stats, exchange(row_stats, "pa", turn), turn, rows)
        if turn < down:
            col_stats = join(col_stats, exchange(col_stats, "pb", turn), turn, rows)
        turn *= 2

    high, low, *blocks, info = weight_sweep(
        scores, even_counts, odd_counts, row_stats, col_stats, even, odd
    )
    even_sum, odd_sum = query_sweep(high, low, passage_slots, info)
    halves = blocks[2::2]
    relayed = [exchange(part, "pb", 1) for part in blocks[3::2]]
    query_sum, term, *sent = middle(
        even_sum, exchange(odd_sum, "pa", 1), info, halves, relayed
    )
    along = [
        exchange(part, "pb", j) for part, j in zip(sent, range(2, down, 2))
    ]
    side = [exchange(part, "pa", k) for part, k in zip(sent[len(along) :], row_turns[1:])]
    near = exchange(blocks[1], "pb", 1)
    grad_passages = finish(blocks[0], along + [near], info, 2)
    grad_queries = finish(query_sum, side, info, 3)
    loss = mean_loss(term, side, along, across * down)
    return (loss.reshape(()), grad_queries, grad_passages)


def solution(mesh):
    return jax.shard_map(
        per_device,
        mesh=mesh,
        in_specs=(
            P(("pb", "pa"), None),
            P(("pb", "pa"), None),
            P(("pb", "pa"), None),
            P(("pb", "pa")),
        ),
        out_specs=(P(), P(("pb", "pa"), None), P(("pb", "pa"), None)),
        check_vma=False,
    )
```

```python
import math

import jax
import jax.numpy as jnp
from jax import lax
from jax.experimental import pallas as pl
from jax.experimental.pallas import tpu as pltpu
from jax.sharding import PartitionSpec as P

F32 = jnp.float32
BF16 = jnp.bfloat16
TIME_BYTES = 3.6e6
VMEM_SPARE = 4 * 1024 * 1024
VMEM_MOST = 56 * 1024 * 1024
CODE_SPAN = 2.0**28
CODE_STEPS = 32000.0 / 28.0
LOSS_UNIT = 1.0 / 4096.0
DIGIT = 2.0**15


def exchange(value, axis, turn):
    size = lax.axis_size(axis)
    return lax.ppermute(value, axis, [(i, i ^ turn) for i in range(size)])


def call(kernel, out_shape, scratch_shapes, *operands, spare=(), room=None, time=0.1):
    size = sum(x.size * x.dtype.itemsize for x in (*operands, *jax.tree.leaves(out_shape)))
    held = [x for x in scratch_shapes if hasattr(x, "memory_space") and x.memory_space == pltpu.VMEM]
    size += sum(math.prod(x.shape) * jnp.dtype(x.dtype).itemsize for x in held)
    spaces = [pl.BlockSpec(memory_space=pltpu.VMEM)] * len(operands)
    spaces += [pl.BlockSpec(memory_space=pl.ANY)] * len(spare)
    return pl.pallas_call(
        kernel,
        out_shape=out_shape,
        in_specs=spaces,
        out_specs=jax.tree.map(lambda _: pl.BlockSpec(memory_space=pltpu.VMEM), out_shape),
        scratch_shapes=scratch_shapes,
        compiler_params=pltpu.CompilerParams(vmem_limit_bytes=room or 2 * size + VMEM_SPARE),
        cost_estimate=pl.CostEstimate(
            flops=1, bytes_accessed=int(time * TIME_BYTES), transcendentals=0
        ),
    )(*operands, *spare)


def put(ref, value):
    rows = value.shape[0]
    for g in range(value.shape[1] // 128):
        ref[g * rows : (g + 1) * rows, :] = value[:, g * 128 : (g + 1) * 128]


def get(ref, rows, width):
    return jnp.concatenate(
        [ref[g * rows : (g + 1) * rows, :] for g in range(width // 128)], axis=1
    )


def first_messages(queries, passages, hard_ids, list_lengths):
    rows, width = queries.shape
    listed = hard_ids.shape[1]
    body = width // 128 * rows
    operands = (passages, hard_ids.T, list_lengths.reshape(1, rows), queries)

    def kernel(*refs):
        sources, (q_out, near_out, far_out), held, sems = refs[:4], refs[4:7], refs[7:11], refs[11]
        copies = [
            pltpu.make_async_copy(src, dst, sems.at[n])
            for n, (src, dst) in enumerate(zip(sources, held))
        ]
        for copy in copies:
            copy.start()
        p_ref, ids_ref, len_ref, q_ref = held
        for copy in copies:
            copy.wait()
        part = p_ref[...].astype(BF16)
        for out in (near_out, far_out):
            put(out, part)
            out[body:, :] = jnp.zeros((out.shape[0] - body, 128), BF16)
        put(q_out, q_ref[...].astype(BF16))
        ids = ids_ref[...].astype(F32)
        live = lax.broadcasted_iota(jnp.int32, (listed, rows), 0) < len_ref[...]
        block = jnp.floor((ids + 0.5) * (1.0 / rows))
        number = (ids - block * rows + 128.0) * jnp.exp2(block - 64.0)
        q_out[body:, :] = jnp.where(live, number, 0.0).astype(BF16)

    return call(
        kernel,
        [jax.ShapeDtypeStruct((body + listed + more, 128), BF16) for more in (0, 0, 16)],
        [pltpu.VMEM(x.shape, x.dtype) for x in operands] + [pltpu.SemaphoreType.DMA((4,))],
        spare=operands,
        room=VMEM_MOST,
        time=2.0,
    )


def count_listed(message, listed, col_slots, after=()):
    body = message.shape[0] - listed
    rows = 128
    row_axis_size = lax.axis_size("pa")

    def kernel(m_ref, *refs):
        count_ref = refs[-1]
        if after:
            refs[-2][...] = m_ref[...]
        down, across = lax.axis_index("pb"), lax.axis_index("pa")
        number = m_ref[body:, :].astype(F32)
        live = number > 0.0
        block = jnp.floor(jnp.log2(jnp.where(live, number, 1.0)) + 57.002)
        inside = (number * jnp.exp2(64.0 - block) - 127.5).astype(jnp.int32)
        block = jnp.where(live, block, -1.0).astype(jnp.int32)
        steps = lax.broadcasted_iota(jnp.int32, (rows, rows), 0)
        for g in range(0, col_slots, 4):
            unit = jnp.zeros((listed, rows), jnp.int32)
            for j in range(g, min(g + 4, col_slots)):
                mine = (down ^ j) * row_axis_size + across
                unit = jnp.where(block == mine, 1 << (8 * (j - g)), unit)
            total = jnp.zeros((rows, rows), jnp.int32)
            for h in range(listed):
                total = total + jnp.where(inside[h : h + 1, :] == steps, unit[h : h + 1, :], 0)
            count_ref[g // 4] = total

    counts = jax.ShapeDtypeStruct((-(-col_slots // 4), rows, rows), jnp.int32)
    if not len(after):
        return message, call(kernel, counts, [], message, time=0.3)
    copied = jax.ShapeDtypeStruct(message.shape, message.dtype)
    return call(kernel, (copied, counts), [], message, spare=after, time=0.3)


def count_at(ref, j):
    return ((ref[j // 4] >> (8 * (j % 4))) & 255).astype(F32)


def score_sweep(messages, passage_slots, counts, rows, width):
    row_slots, col_slots = len(messages), len(passage_slots)
    tall, wide = row_slots * rows, col_slots * rows

    def most_of(part):
        most = jnp.max(jnp.abs(part.astype(F32)), axis=0, keepdims=True)
        return jnp.max(most, axis=1, keepdims=True)

    def kernel(*refs):
        q_refs, refs = refs[:row_slots], refs[row_slots:]
        p_refs, refs = refs[:col_slots], refs[col_slots:]
        c_refs, refs = refs[:row_slots], refs[row_slots:]
        s_ref, stat_ref, q_all, p_all, top_acc = refs
        stat_ref[...] = jnp.zeros_like(stat_ref)
        passage_most = jnp.zeros((1, 1), F32)
        for j in range(col_slots):
            part = get(p_refs[j], rows, width)
            p_all[j * rows : (j + 1) * rows, :] = part
            passage_most = jnp.maximum(passage_most, most_of(part))
        query_most = jnp.zeros((1, 1), F32)
        for m in range(row_slots // 2):
            both = [get(q, rows, width) for q in q_refs[2 * m : 2 * m + 2]]
            both = jnp.concatenate(both, axis=0)
            query_most = jnp.maximum(query_most, most_of(both))
            spot = slice(2 * m * rows, 2 * (m + 1) * rows)
            q_all[spot, :] = both
            s_ref[:, spot] = lax.dot_general(
                p_all[...], both, (((1,), (1,)), ((), ())), preferred_element_type=F32
            )
        stat_ref[2:3, :tall] = jnp.broadcast_to(passage_most, (1, tall))
        stat_ref[2:3, tall:] = jnp.broadcast_to(query_most, (1, wide))
        unit = lax.broadcasted_iota(jnp.int32, (rows, rows), 0) == lax.broadcasted_iota(
            jnp.int32, (rows, rows), 1
        )
        pairs = jnp.sum(jnp.where(unit, s_ref[:rows, :rows], 0.0), axis=0, keepdims=True)
        stat_ref[3:4, :tall] = jnp.broadcast_to(
            jnp.sum(pairs, axis=1, keepdims=True), (1, tall)
        )
        for k in range(row_slots):
            spot = slice(k * rows, (k + 1) * rows)
            top = jnp.full((1, rows), -jnp.inf, F32)
            for j in range(col_slots):
                here = slice(j * rows, (j + 1) * rows)
                part = s_ref[here, spot]
                top = jnp.maximum(top, jnp.max(part, axis=0, keepdims=True))
                if k == 0:
                    top_acc[here, :] = part
                else:
                    top_acc[here, :] = jnp.maximum(top_acc[here, :], part)
            total = jnp.zeros((1, rows), F32)
            for j in range(col_slots):
                here = slice(j * rows, (j + 1) * rows)
                times = 1.0 + count_at(c_refs[k], j)
                total = total + jnp.sum(
                    jnp.exp(s_ref[here, spot] - top) * times, axis=0, keepdims=True
                )
            stat_ref[0:1, spot] = top
            stat_ref[1:2, spot] = total
        for j in range(col_slots):
            here = slice(j * rows, (j + 1) * rows)
            there = slice(tall + j * rows, tall + (j + 1) * rows)
            acc = top_acc[here, :]
            stat_ref[0:1, there] = jnp.max(acc.T, axis=0, keepdims=True)
            top = jnp.max(acc, axis=1, keepdims=True)
            total = jnp.zeros((rows, rows), F32)
            for k in range(row_slots):
                total = total + jnp.exp(s_ref[here, k * rows : (k + 1) * rows] - top)
            stat_ref[1:2, there] = jnp.sum(total.T, axis=0, keepdims=True)

    return call(
        kernel,
        (
            jax.ShapeDtypeStruct((wide, tall), F32),
            jax.ShapeDtypeStruct((8, tall + wide), F32),
            jax.ShapeDtypeStruct((tall, width), BF16),
            jax.ShapeDtypeStruct((wide, width), BF16),
        ),
        [pltpu.VMEM((wide, rows), F32)],
        *messages,
        *passage_slots,
        *counts,
        time=2.0,
    )


def turned(value, turn, rows):
    slots = value.shape[1] // rows
    return jnp.concatenate(
        [value[:, (k ^ turn) * rows : ((k ^ turn) + 1) * rows] for k in range(slots)], axis=1
    )


def tree(combine, values):
    while len(values) > 1:
        values = [combine(a, b) for a, b in zip(values[::2], values[1::2])]
    return values[0]


def joined(one, two):
    top = jnp.maximum(one[0:1], two[0:1])
    total = one[1:2] * jnp.exp(one[0:1] - top) + two[1:2] * jnp.exp(two[0:1] - top)
    most = jnp.maximum(one[2:3], two[2:3])
    return jnp.concatenate([top, total, most, one[3:] + two[3:]], axis=0)


def share_out(own, other, tall, wide, rows, after):
    def kernel(own_ref, other_ref, after_ref, out_ref):
        first = lax.axis_index("pa") % 2 == 0
        by_row = joined(own_ref[:, :tall], turned(other_ref[:, :tall], 1, rows))
        by_col = jnp.concatenate([own_ref[:, tall:], other_ref[:, tall:]], axis=1)
        out_ref[...] = jnp.where(first, by_row, by_col)

    return call(kernel, jax.ShapeDtypeStruct((8, tall), F32), [], own, other, spare=[after])


def share_all(own, others, rows):
    def kernel(own_ref, *refs):
        first = lax.axis_index("pa") % 2 == 0
        parts = [own_ref[...]]
        for t, ref in enumerate(refs[:-1], start=1):
            there = ref[...]
            parts.append(jnp.where(first, turned(there, 2 * t, rows), turned(there, t, rows)))
        refs[-1][...] = tree(joined, parts)

    return call(kernel, jax.ShapeDtypeStruct(own.shape, F32), [], own, *others)


def levels(own, other, wide, rows):
    tall = own.shape[1]

    def kernel(own_ref, other_ref, row_ref, col_ref, info_ref):
        first = lax.axis_index("pa") % 2 == 0
        own_v, other_v = own_ref[...], other_ref[...]
        by_row = jnp.where(first, own_v, turned(other_v, 1, rows))
        by_col = jnp.where(first, other_v, own_v)
        mine = jnp.where(first, by_col[:, wide:], by_col[:, :wide])
        row_level = by_row[0:1] + jnp.log(by_row[1:2])
        both = by_col[0:1] + jnp.log(by_col[1:2])
        row_ref[...] = jnp.broadcast_to(row_level, row_ref.shape)
        columns = mine[0:1] + jnp.log(mine[1:2])
        for j in range(wide // rows):
            here = slice(j * rows, (j + 1) * rows)
            col_ref[here, :] = jnp.broadcast_to(columns[:, here], (rows, rows)).T

        def summed(level):
            parts = [
                jnp.sum(level[:, g * rows : (g + 1) * rows], axis=1, keepdims=True)
                for g in range(level.shape[1] // rows)
            ]
            return tree(jnp.add, parts)

        row_term = summed(row_level) - 2.0 * by_row[3:4, :1]
        query_bound = jnp.maximum(mine[2:3, :1] * (tall * 1.02 + 8.0), 1e-30)
        passage_bound = jnp.maximum(by_row[2:3, :1] * (2 * wide * 1.02 + 8.0), 1e-30)
        info_ref[...] = jnp.zeros_like(info_ref)
        for n, value in enumerate((row_term, summed(both), query_bound, passage_bound)):
            info_ref[n : n + 1, :] = jnp.broadcast_to(value, (1, rows))

    return call(
        kernel,
        (
            jax.ShapeDtypeStruct((8, tall), F32),
            jax.ShapeDtypeStruct((wide, rows), F32),
            jax.ShapeDtypeStruct((8, rows), F32),
        ),
        [],
        own,
        other,
    )


def coded(value, inverse):
    steps = jnp.log2(jnp.abs(value) * (inverse * CODE_SPAN) + 1.0) * CODE_STEPS + 0.5
    return jnp.where(value < 0.0, -steps, steps).astype(jnp.int32).astype(jnp.int16)


def decoded(code, bound):
    steps = code.astype(F32)
    size = (jnp.exp2(jnp.abs(steps) * (1.0 / CODE_STEPS)) - 1.0) * (bound * (1.0 / CODE_SPAN))
    return jnp.where(steps < 0.0, -size, size)


def write_term(ref, value):
    lanes = lax.broadcasted_iota(jnp.int32, (16, 128), 1)
    left = value[:, :1] * LOSS_UNIT
    digits = jnp.zeros((16, 128), F32)
    for n in range(3):
        digit = jnp.round(left)
        left = (left - digit) * DIGIT
        digits = jnp.where(lanes == n, digit, digits)
    ref[ref.shape[0] - 16 :, :] = digits.astype(jnp.int32).astype(jnp.int16)


def read_term(ref):
    digits = ref[ref.shape[0] - 16 :, :].astype(F32)[:1, :]
    one, two, three = digits[:, 0:1], digits[:, 1:2], digits[:, 2:3]
    return (one + (two + three * (1.0 / DIGIT)) * (1.0 / DIGIT)) * (1.0 / LOSS_UNIT)


def weight_sweep(picked, scores, row_level, col_level, counts):
    wide, tall = scores.shape
    rows = col_level.shape[1]
    row_slots = tall // rows

    def kernel(s_ref, row_ref, col_ref, *refs):
        c_refs, (hi_ref, lo_ref) = refs[:row_slots], refs[row_slots:]
        unit = (
            lax.broadcasted_iota(jnp.int32, (rows, rows), 0)
            == lax.broadcasted_iota(jnp.int32, (rows, rows), 1)
        ).astype(F32)
        for n, j in enumerate(picked):
            here = slice(j * rows, (j + 1) * rows)
            for k in range(row_slots):
                spot = slice(k * rows, (k + 1) * rows)
                part = s_ref[here, spot]
                by_row = jnp.exp(part - row_ref[0:1, spot])
                by_col = jnp.exp(part - col_ref[here, :])
                pair = (by_row + by_col).astype(BF16).astype(F32)
                hard = by_row.astype(BF16).astype(F32)
                weight = pair + hard * count_at(c_refs[k], j)
                if j == 0 and k == 0:
                    weight = weight - 2.0 * unit
                high = weight.astype(BF16)
                hi_ref[n, :, spot] = high
                lo_ref[n, :, spot] = (weight - high.astype(F32)).astype(BF16)

    weights = jax.ShapeDtypeStruct((len(picked), rows, tall), BF16)
    return call(
        kernel,
        (weights, weights),
        [],
        scores,
        row_level,
        col_level,
        *counts,
        time=0.45 * len(picked),
    )


def passage_sweep(picked, held, weights, q_all, info, term=False):
    high, low = weights
    rows, width = info.shape[1], q_all.shape[1]
    body = width // 128 * rows
    odd = [j for j in picked if j % 2]
    even = [j for j in picked if j % 2 == 0]

    def kernel(hi_ref, lo_ref, q_ref, info_ref, *out_refs):
        inverse = 1.0 / info_ref[2:3, :1]
        if term:
            write_term(out_refs[-1], info_ref[0:1, :])
        for j in picked:
            n = held.index(j)
            part = jnp.dot(hi_ref[n], q_ref[...], preferred_element_type=F32)
            part = part + jnp.dot(lo_ref[n], q_ref[...], preferred_element_type=F32)
            if j % 2:
                first = odd.index(j) * body
                put(out_refs[-1].at[first : first + body, :], coded(part, inverse))
            else:
                put(out_refs[even.index(j)], part)

    outs = [jax.ShapeDtypeStruct((body, 128), F32)] * len(even)
    if odd:
        outs.append(jax.ShapeDtypeStruct((len(odd) * body + 16 * term, 128), jnp.int16))
    return call(kernel, outs, [], high, low, q_all, info, time=0.4 * len(picked))


def flipped(block):
    def kernel(in_ref, out_ref):
        out_ref[...] = in_ref[...].astype(F32).T.astype(BF16)

    shape = jax.ShapeDtypeStruct(block.shape[::-1], BF16)
    return call(kernel, shape, [], block, time=0.3)


def query_sweep(pairs, weights, picked, passages, info):
    width, rows = passages.shape[0], info.shape[1]
    slots = sorted((j, 2 * i, n) for i, part in enumerate(picked) for n, j in enumerate(part))

    def kernel(*refs):
        w_refs, (p_ref, info_ref, *even_refs, odd_ref) = refs[: len(weights)], refs[len(weights) :]
        for i, (m, even_ref) in enumerate(zip(pairs, even_refs)):
            spot = slice(2 * m * rows, 2 * (m + 1) * rows)
            total = jnp.zeros((width, 2 * rows), F32)
            for side in range(2):
                weight = [w_refs[g + side][n, :, spot] for _, g, n in slots]
                weight = jnp.concatenate(weight, axis=0)
                total = total + jnp.dot(p_ref[...], weight, preferred_element_type=F32)
            even_ref[...] = total[:, :rows]
            odd_ref[i * width : (i + 1) * width, :] = coded(
                total[:, rows:], 1.0 / info_ref[3:4, :1]
            )

    blocks = [jax.ShapeDtypeStruct((width, rows), F32)] * len(pairs)
    blocks.append(jax.ShapeDtypeStruct((len(pairs) * width, rows), jnp.int16))
    return call(kernel, blocks, [], *weights, passages, info, time=0.6 * len(pairs))


def send_on(own, arrived, info, bound_row, term_row, part=0, longer=0, after=()):
    body = own.shape[0]

    def kernel(own_ref, arrived_ref, info_ref, *refs):
        out_ref = refs[-1]
        bound = info_ref[bound_row : bound_row + 1, :1]
        total = own_ref[...] + decoded(arrived_ref[part * body : (part + 1) * body, :], bound)
        out_ref[:body, :] = coded(total, 1.0 / bound)
        out_ref[body:, :] = jnp.zeros((16 + longer, 128), jnp.int16)
        term = info_ref[term_row : term_row + 1, :1]
        if arrived.shape[0] % body:
            term = term + read_term(arrived_ref)
        write_term(out_ref, term)

    return call(
        kernel,
        jax.ShapeDtypeStruct((body + 16 + longer, 128), jnp.int16),
        [],
        own,
        arrived,
        info,
        spare=after,
        time=0.5,
    )


def added(own, arrived, info, bound_row, after=()):
    body = own.shape[0]

    def kernel(own_ref, info_ref, *refs):
        bound = info_ref[bound_row : bound_row + 1, :1]
        total = own_ref[...]
        for (_, part), ref in zip(arrived, refs):
            total = total + decoded(ref[part * body : (part + 1) * body, :], bound)
        refs[-1][...] = total

    block = jax.ShapeDtypeStruct(own.shape, F32)
    messages = [message for message, _ in arrived]
    return call(kernel, block, [], own, info, *messages, spare=after, time=0.3)


def finish_passages(own, arrived, info, width, after):
    body = own.shape[0]
    rows = body * 128 // width

    def kernel(own_ref, info_ref, *refs):
        bound = info_ref[2:3, :1]
        total = own_ref[...]
        for ref in refs[: len(arrived)]:
            total = total + decoded(ref[:body, :], bound)
        refs[-2][...] = 0.5 * get(total, rows, width)
        refs[-1][...] = info_ref[...]

    outs = (jax.ShapeDtypeStruct((rows, width), F32), jax.ShapeDtypeStruct(info.shape, F32))
    return call(kernel, outs, [], own, info, *arrived, spare=after, time=1.0)


def finish_queries(own, late, side, near, along, info, devices, after):
    body, rows = own.shape

    def kernel(own_ref, info_ref, term_ref, *refs):
        s_refs, refs = refs[: len(side)], refs[len(side) :]
        a_refs, (loss_ref, out_ref) = refs[: len(along)], refs[-2:]
        bound = info_ref[3:4, :1]
        total = own_ref[...]
        for ref in s_refs[:late]:
            total = total + decoded(ref[:body, :], bound)
        for g in range(body // 128):
            here = slice(g * 128, (g + 1) * 128)
            out_ref[:, here] = 0.5 * total[here, :].T
        sides = [info_ref[1:2, :1]] + [read_term(ref) for ref in s_refs]
        lines = [info_ref[0:1, :1] + read_term(term_ref)] + [read_term(ref) for ref in a_refs]
        loss = tree(jnp.add, sides) + tree(jnp.add, lines)
        loss_ref[...] = loss * (1.0 / (2.0 * rows * devices))

    outs = (jax.ShapeDtypeStruct((1, 1), F32), jax.ShapeDtypeStruct((rows, body), F32))
    return call(kernel, outs, [], own, info, near, *side, *along, spare=[after], time=1.0)


def per_device(queries, passages, hard_ids, list_lengths):
    rows, width = queries.shape
    listed = hard_ids.shape[1]
    across = lax.axis_size("pa")
    down = lax.axis_size("pb")
    tall, wide = across * rows, down * rows

    message, near_message, far_message = first_messages(
        queries, passages, hard_ids, list_lengths
    )
    far = [exchange(far_message, "pb", j) for j in range(2, down, 2)]
    near = exchange(near_message, "pb", 1)
    passage_slots = [near_message, near]
    for part in far:
        passage_slots += [part, exchange(part, "pb", 1)]
    row_turns = list(range(0, across, 2))
    messages, counts = [], []
    for k in row_turns:
        part = exchange(message, "pa", k) if k else message
        part, count = count_listed(part, listed, down, [near, *far, counts[0]] if k else [])
        other, other_count = count_listed(exchange(part, "pa", 1), listed, down)
        messages += [part, other]
        counts += [count, other_count]

    scores, stats, q_all, p_all = score_sweep(messages, passage_slots, counts, rows, width)
    passages = flipped(p_all)
    stats = share_out(stats, exchange(stats, "pa", 1), tall, wide, rows, passages)
    others = []
    for t in range(1, down):
        pairs = []
        for i in range(across * down):
            z, c = divmod(i, across)
            pairs.append((i, z * across + (c ^ 2 * t) if c % 2 == 0 else (z ^ t) * across + c))
        others.append(lax.ppermute(stats, ("pb", "pa"), pairs))
    stats = share_all(stats, others, rows)
    row_level, col_level, info = levels(stats, exchange(stats, "pa", 1), wide, rows)

    swept = (scores, row_level, col_level, counts)
    onward = list(range(3, down, 2))
    staying = [*range(2, down, 2), 1, 0]
    first = weight_sweep(onward, *swept)
    (near,) = passage_sweep(onward, onward, first, q_all, info, True)
    near = exchange(near, "pb", 1)
    second = weight_sweep(staying, *swept)
    weights = [*first, *second]
    blocks = passage_sweep(staying[:-2], staying, second, q_all, info)
    along = [
        exchange(send_on(own, near, info, 2, 0, part, 16), "pb", 2 * (part + 1))
        for part, own in enumerate(blocks)
    ]
    (last,) = passage_sweep([1], staying, second, q_all, info)
    last = exchange(last, "pb", 1)
    (passage_sum,) = passage_sweep([0], staying, second, q_all, info)

    side = []
    for m in range(across // 2):
        own, other = query_sweep([m], weights, [onward, staying], passages, info)
        other = exchange(other, "pa", 1)
        if m:
            after = [last] if m == 2 else []
            side.append(exchange(send_on(own, other, info, 3, 1, after=after), "pa", 2 * m))
        else:
            query_sum, core = own, other
    query_sum = added(query_sum, [(core, 0), (side[-1], 0)], info, 3)
    grad_passages, after = finish_passages(
        passage_sum, [last, *along], info, width, [query_sum]
    )
    loss, grad_queries = finish_queries(
        query_sum, len(side) - 1, side, near, along, info, across * down, after
    )
    return (loss.reshape(()), grad_queries, grad_passages)


def solution(mesh):
    return jax.shard_map(
        per_device,
        mesh=mesh,
        in_specs=(
            P(("pb", "pa"), None),
            P(("pb", "pa"), None),
            P(("pb", "pa"), None),
            P(("pb", "pa")),
        ),
        out_specs=(P(), P(("pb", "pa"), None), P(("pb", "pa"), None)),
        check_vma=False,
    )
```

```python
import math

import jax
import jax.numpy as jnp
from jax import lax
from jax.experimental import pallas as pl
from jax.experimental.pallas import tpu as pltpu
from jax.sharding import PartitionSpec as P

F32 = jnp.float32
BF16 = jnp.bfloat16
TIME_BYTES = 3.6e6
VMEM_SPARE = 4 * 1024 * 1024
VMEM_MOST = 56 * 1024 * 1024
CODE_SPAN = 2.0**28
CODE_STEPS = 32000.0 / 28.0
LOSS_UNIT = 1.0 / 16384.0
DIGIT = 2.0**15


def exchange(value, axis, turn):
    size = lax.axis_size(axis)
    return lax.ppermute(value, axis, [(i, i ^ turn) for i in range(size)])


def call(kernel, out_shape, scratch_shapes, *operands, spare=(), room=None, time=0.1):
    size = sum(x.size * x.dtype.itemsize for x in (*operands, *jax.tree.leaves(out_shape)))
    held = [x for x in scratch_shapes if hasattr(x, "memory_space") and x.memory_space == pltpu.VMEM]
    size += sum(math.prod(x.shape) * jnp.dtype(x.dtype).itemsize for x in held)
    spaces = [pl.BlockSpec(memory_space=pltpu.VMEM)] * len(operands)
    spaces += [pl.BlockSpec(memory_space=pl.ANY)] * len(spare)
    return pl.pallas_call(
        kernel,
        out_shape=out_shape,
        in_specs=spaces,
        out_specs=jax.tree.map(lambda _: pl.BlockSpec(memory_space=pltpu.VMEM), out_shape),
        scratch_shapes=scratch_shapes,
        compiler_params=pltpu.CompilerParams(vmem_limit_bytes=room or 2 * size + VMEM_SPARE),
        cost_estimate=pl.CostEstimate(
            flops=1, bytes_accessed=int(time * TIME_BYTES), transcendentals=0
        ),
    )(*operands, *spare)


def put(ref, value):
    rows = value.shape[0]
    for g in range(value.shape[1] // 128):
        ref[g * rows : (g + 1) * rows, :] = value[:, g * 128 : (g + 1) * 128]


def get(ref, rows, width):
    return jnp.concatenate(
        [ref[g * rows : (g + 1) * rows, :] for g in range(width // 128)], axis=1
    )


def first_messages(queries, passages, hard_ids, list_lengths):
    rows, width = queries.shape
    listed = hard_ids.shape[1]
    body = width // 128 * rows
    operands = (passages, hard_ids.T, list_lengths.reshape(1, rows), queries)

    def kernel(*refs):
        sources, (q_out, near_out, far_out), held, sems = refs[:4], refs[4:7], refs[7:11], refs[11]
        copies = [
            pltpu.make_async_copy(src, dst, sems.at[n])
            for n, (src, dst) in enumerate(zip(sources, held))
        ]
        for copy in copies:
            copy.start()
        p_ref, ids_ref, len_ref, q_ref = held
        for copy in copies:
            copy.wait()
        part = p_ref[...].astype(BF16)
        for out in (near_out, far_out):
            put(out, part)
            out[body:, :] = jnp.zeros((out.shape[0] - body, 128), BF16)
        put(q_out, q_ref[...].astype(BF16))
        ids = ids_ref[...].astype(F32)
        live = lax.broadcasted_iota(jnp.int32, (listed, rows), 0) < len_ref[...]
        block = jnp.floor((ids + 0.5) * (1.0 / rows))
        number = (ids - block * rows + 128.0) * jnp.exp2(block - 64.0)
        q_out[body:, :] = jnp.where(live, number, 0.0).astype(BF16)

    return call(
        kernel,
        [jax.ShapeDtypeStruct((body + listed + more, 128), BF16) for more in (0, 0, 16)],
        [pltpu.VMEM(x.shape, x.dtype) for x in operands] + [pltpu.SemaphoreType.DMA((4,))],
        spare=operands,
        room=VMEM_MOST,
        time=2.0,
    )


def count_listed(message, listed, col_slots, after=()):
    body = message.shape[0] - listed
    rows = 128
    row_axis_size = lax.axis_size("pa")

    def kernel(m_ref, *refs):
        count_ref = refs[-1]
        if after:
            refs[-2][...] = m_ref[...]
        down, across = lax.axis_index("pb"), lax.axis_index("pa")
        number = m_ref[body:, :].astype(F32)
        live = number > 0.0
        block = jnp.floor(jnp.log2(jnp.where(live, number, 1.0)) + 57.002)
        inside = (number * jnp.exp2(64.0 - block) - 127.5).astype(jnp.int32)
        block = jnp.where(live, block, -1.0).astype(jnp.int32)
        steps = lax.broadcasted_iota(jnp.int32, (rows, rows), 0)
        for g in range(0, col_slots, 4):
            unit = jnp.zeros((listed, rows), jnp.int32)
            for j in range(g, min(g + 4, col_slots)):
                mine = (down ^ j) * row_axis_size + across
                unit = jnp.where(block == mine, 1 << (8 * (j - g)), unit)
            total = jnp.zeros((rows, rows), jnp.int32)
            for h in range(listed):
                total = total + jnp.where(inside[h : h + 1, :] == steps, unit[h : h + 1, :], 0)
            count_ref[g // 4] = total

    counts = jax.ShapeDtypeStruct((-(-col_slots // 4), rows, rows), jnp.int32)
    if not len(after):
        return message, call(kernel, counts, [], message, time=0.3)
    copied = jax.ShapeDtypeStruct(message.shape, message.dtype)
    return call(kernel, (copied, counts), [], message, spare=after, time=0.3)


def count_at(ref, j):
    return ((ref[j // 4] >> (8 * (j % 4))) & 255).astype(F32)


def score_sweep(messages, passage_slots, counts, rows, width):
    row_slots, col_slots = len(messages), len(passage_slots)
    tall, wide = row_slots * rows, col_slots * rows

    def most_of(part):
        tiles = [jnp.abs(part[n : n + 16, :]) for n in range(0, part.shape[0], 16)]
        most = jnp.max(tree(jnp.maximum, tiles).astype(F32), axis=0, keepdims=True)
        return jnp.max(most, axis=1, keepdims=True)

    def kernel(*refs):
        q_refs, refs = refs[:row_slots], refs[row_slots:]
        p_refs, refs = refs[:col_slots], refs[col_slots:]
        c_refs, refs = refs[:row_slots], refs[row_slots:]
        s_ref, stat_ref, q_all, p_all, top_acc = refs
        stat_ref[...] = jnp.zeros_like(stat_ref)
        passage_most = jnp.zeros((1, 1), F32)
        for j in range(col_slots):
            part = get(p_refs[j], rows, width)
            p_all[j * rows : (j + 1) * rows, :] = part
            passage_most = jnp.maximum(passage_most, most_of(part))
        def row_stats(k):
            spot = slice(k * rows, (k + 1) * rows)
            tops = []
            for j in range(col_slots):
                here = slice(j * rows, (j + 1) * rows)
                part = s_ref[here, spot]
                tops.append(jnp.max(part, axis=0, keepdims=True))
                if k == 0:
                    top_acc[here, :] = part
                else:
                    top_acc[here, :] = jnp.maximum(top_acc[here, :], part)
            top = tree(jnp.maximum, tops)
            total = jnp.zeros((rows, rows), F32)
            for j in range(col_slots):
                here = slice(j * rows, (j + 1) * rows)
                times = 1.0 + count_at(c_refs[k], j)
                total = total + jnp.exp(s_ref[here, spot] - top) * times
            stat_ref[0:1, spot] = top
            stat_ref[1:2, spot] = jnp.sum(total, axis=0, keepdims=True)

        query_most = jnp.zeros((1, 1), F32)
        for m in range(row_slots // 2):
            both = [get(q, rows, width) for q in q_refs[2 * m : 2 * m + 2]]
            both = jnp.concatenate(both, axis=0)
            query_most = jnp.maximum(query_most, most_of(both))
            spot = slice(2 * m * rows, 2 * (m + 1) * rows)
            q_all[spot, :] = both
            s_ref[:, spot] = lax.dot_general(
                p_all[...], both, (((1,), (1,)), ((), ())), preferred_element_type=F32
            )
            if m:
                row_stats(2 * m - 2)
                row_stats(2 * m - 1)
        row_stats(row_slots - 2)
        row_stats(row_slots - 1)
        stat_ref[2:3, :tall] = jnp.broadcast_to(passage_most, (1, tall))
        stat_ref[2:3, tall:] = jnp.broadcast_to(query_most, (1, wide))
        unit = lax.broadcasted_iota(jnp.int32, (rows, rows), 0) == lax.broadcasted_iota(
            jnp.int32, (rows, rows), 1
        )
        pairs = jnp.sum(jnp.where(unit, s_ref[:rows, :rows], 0.0), axis=0, keepdims=True)
        stat_ref[3:4, :rows] = pairs
        stat_ref[3:4, tall : tall + rows] = pairs
        for j in range(col_slots):
            here = slice(j * rows, (j + 1) * rows)
            there = slice(tall + j * rows, tall + (j + 1) * rows)
            acc = top_acc[here, :]
            stat_ref[0:1, there] = jnp.max(acc.T, axis=0, keepdims=True)
            top = jnp.max(acc, axis=1, keepdims=True)
            total = jnp.zeros((rows, rows), F32)
            for k in range(row_slots):
                total = total + jnp.exp(s_ref[here, k * rows : (k + 1) * rows] - top)
            stat_ref[1:2, there] = jnp.sum(total.T, axis=0, keepdims=True)

    return call(
        kernel,
        (
            jax.ShapeDtypeStruct((wide, tall), F32),
            jax.ShapeDtypeStruct((8, tall + wide), F32),
            jax.ShapeDtypeStruct((tall, width), BF16),
            jax.ShapeDtypeStruct((wide, width), BF16),
        ),
        [pltpu.VMEM((wide, rows), F32)],
        *messages,
        *passage_slots,
        *counts,
        time=2.0,
    )


def turned(value, turn, rows):
    slots = value.shape[1] // rows
    return jnp.concatenate(
        [value[:, (k ^ turn) * rows : ((k ^ turn) + 1) * rows] for k in range(slots)], axis=1
    )


def tree(combine, values):
    while len(values) > 1:
        values = [combine(a, b) for a, b in zip(values[::2], values[1::2])]
    return values[0]


def joined(one, two):
    top = jnp.maximum(one[0:1], two[0:1])
    total = one[1:2] * jnp.exp(one[0:1] - top) + two[1:2] * jnp.exp(two[0:1] - top)
    most = jnp.maximum(one[2:3], two[2:3])
    return jnp.concatenate([top, total, most, one[3:] + two[3:]], axis=0)


def share_out(own, other, tall, wide, rows, after):
    def kernel(own_ref, other_ref, after_ref, out_ref):
        first = lax.axis_index("pa") % 2 == 0
        by_row = joined(own_ref[:, :tall], turned(other_ref[:, :tall], 1, rows))
        by_col = jnp.concatenate([own_ref[:, tall:], other_ref[:, tall:]], axis=1)
        out_ref[...] = jnp.where(first, by_row, by_col)

    return call(kernel, jax.ShapeDtypeStruct((8, tall), F32), [], own, other, spare=[after])


def share_all(own, others, rows):
    def kernel(own_ref, *refs):
        first = lax.axis_index("pa") % 2 == 0
        parts = [own_ref[...]]
        for t, ref in enumerate(refs[:-1], start=1):
            there = ref[...]
            parts.append(jnp.where(first, turned(there, 2 * t, rows), turned(there, t, rows)))
        refs[-1][...] = tree(joined, parts)

    return call(kernel, jax.ShapeDtypeStruct(own.shape, F32), [], own, *others)


def levels(own, other, wide, rows):
    tall = own.shape[1]

    def kernel(own_ref, other_ref, row_ref, col_ref, info_ref):
        first = lax.axis_index("pa") % 2 == 0
        own_v, other_v = own_ref[...], other_ref[...]
        by_row = jnp.where(first, own_v, turned(other_v, 1, rows))
        by_col = jnp.where(first, other_v, own_v)
        mine = jnp.where(first, by_col[:, wide:], by_col[:, :wide])
        row_level = by_row[0:1] + jnp.log(by_row[1:2])
        both = by_col[0:1] + jnp.log(by_col[1:2])
        row_ref[...] = jnp.broadcast_to(row_level, row_ref.shape)
        columns = mine[0:1] + jnp.log(mine[1:2])
        for j in range(wide // rows):
            here = slice(j * rows, (j + 1) * rows)
            col_ref[here, :] = jnp.broadcast_to(columns[:, here], (rows, rows)).T

        def summed(level):
            parts = [
                jnp.sum(level[:, g * rows : (g + 1) * rows], axis=1, keepdims=True)
                for g in range(level.shape[1] // rows)
            ]
            return tree(jnp.add, parts)

        row_term = summed(row_level - by_row[3:4])
        col_term = summed(both - by_col[3:4])
        query_bound = jnp.maximum(mine[2:3, :1] * (tall * 1.02 + 8.0), 1e-30)
        passage_bound = jnp.maximum(by_row[2:3, :1] * (2 * wide * 1.02 + 8.0), 1e-30)
        info_ref[...] = jnp.zeros_like(info_ref)
        for n, value in enumerate((row_term, col_term, query_bound, passage_bound)):
            info_ref[n : n + 1, :] = jnp.broadcast_to(value, (1, rows))

    return call(
        kernel,
        (
            jax.ShapeDtypeStruct((8, tall), F32),
            jax.ShapeDtypeStruct((wide, rows), F32),
            jax.ShapeDtypeStruct((8, rows), F32),
        ),
        [],
        own,
        other,
    )


def coded(value, inverse):
    steps = jnp.log2(jnp.abs(value) * (inverse * CODE_SPAN) + 1.0) * CODE_STEPS + 0.5
    return jnp.where(value < 0.0, -steps, steps).astype(jnp.int32).astype(jnp.int16)


def decoded(code, bound):
    steps = code.astype(F32)
    size = (jnp.exp2(jnp.abs(steps) * (1.0 / CODE_STEPS)) - 1.0) * (bound * (1.0 / CODE_SPAN))
    return jnp.where(steps < 0.0, -size, size)


def write_term(ref, value):
    lanes = lax.broadcasted_iota(jnp.int32, (16, 128), 1)
    left = value[:, :1] * LOSS_UNIT
    digits = jnp.zeros((16, 128), F32)
    for n in range(3):
        digit = jnp.round(left)
        left = (left - digit) * DIGIT
        digits = jnp.where(lanes == n, digit, digits)
    ref[ref.shape[0] - 16 :, :] = digits.astype(jnp.int32).astype(jnp.int16)


def read_term(ref):
    digits = ref[ref.shape[0] - 16 :, :].astype(F32)[:1, :]
    one, two, three = digits[:, 0:1], digits[:, 1:2], digits[:, 2:3]
    return (one + (two + three * (1.0 / DIGIT)) * (1.0 / DIGIT)) * (1.0 / LOSS_UNIT)


def weight_sweep(picked, scores, row_level, col_level, counts):
    wide, tall = scores.shape
    rows = col_level.shape[1]
    row_slots = tall // rows

    def kernel(s_ref, row_ref, col_ref, *refs):
        c_refs, (hi_ref, lo_ref) = refs[:row_slots], refs[row_slots:]
        unit = (
            lax.broadcasted_iota(jnp.int32, (rows, rows), 0)
            == lax.broadcasted_iota(jnp.int32, (rows, rows), 1)
        ).astype(F32)
        for n, j in enumerate(picked):
            here = slice(j * rows, (j + 1) * rows)
            for k in range(row_slots):
                spot = slice(k * rows, (k + 1) * rows)
                part = s_ref[here, spot]
                by_row = jnp.exp(part - row_ref[0:1, spot])
                by_col = jnp.exp(part - col_ref[here, :])
                pair = (by_row + by_col).astype(BF16).astype(F32)
                hard = by_row.astype(BF16).astype(F32)
                weight = pair + hard * count_at(c_refs[k], j)
                if j == 0 and k == 0:
                    weight = weight - 2.0 * unit
                high = weight.astype(BF16)
                hi_ref[n, :, spot] = high
                lo_ref[n, :, spot] = (weight - high.astype(F32)).astype(BF16)

    weights = jax.ShapeDtypeStruct((len(picked), rows, tall), BF16)
    return call(
        kernel,
        (weights, weights),
        [],
        scores,
        row_level,
        col_level,
        *counts,
        time=0.45 * len(picked),
    )


def passage_sweep(picked, held, weights, q_all, info, term=False):
    high, low = weights
    rows, width = info.shape[1], q_all.shape[1]
    body = width // 128 * rows
    odd = [j for j in picked if j % 2]
    even = [j for j in picked if j % 2 == 0]

    def kernel(hi_ref, lo_ref, q_ref, info_ref, *out_refs):
        inverse = 1.0 / info_ref[2:3, :1]
        if term:
            write_term(out_refs[-1], info_ref[0:1, :])
        for j in picked:
            n = held.index(j)
            part = jnp.dot(hi_ref[n], q_ref[...], preferred_element_type=F32)
            part = part + jnp.dot(lo_ref[n], q_ref[...], preferred_element_type=F32)
            if j % 2:
                first = odd.index(j) * body
                put(out_refs[-1].at[first : first + body, :], coded(part, inverse))
            else:
                put(out_refs[even.index(j)], part)

    outs = [jax.ShapeDtypeStruct((body, 128), F32)] * len(even)
    if odd:
        outs.append(jax.ShapeDtypeStruct((len(odd) * body + 16 * term, 128), jnp.int16))
    return call(kernel, outs, [], high, low, q_all, info, time=0.4 * len(picked))


def flipped(block):
    def kernel(in_ref, out_ref):
        out_ref[...] = in_ref[...].astype(F32).T.astype(BF16)

    shape = jax.ShapeDtypeStruct(block.shape[::-1], BF16)
    return call(kernel, shape, [], block, time=0.3)


def query_sweep(pairs, weights, picked, passages, info):
    width, rows = passages.shape[0], info.shape[1]
    slots = sorted((j, 2 * i, n) for i, part in enumerate(picked) for n, j in enumerate(part))

    def kernel(*refs):
        w_refs, (p_ref, info_ref, *even_refs, odd_ref) = refs[: len(weights)], refs[len(weights) :]
        for i, (m, even_ref) in enumerate(zip(pairs, even_refs)):
            spot = slice(2 * m * rows, 2 * (m + 1) * rows)
            total = jnp.zeros((width, 2 * rows), F32)
            for side in range(2):
                weight = [w_refs[g + side][n, :, spot] for _, g, n in slots]
                weight = jnp.concatenate(weight, axis=0)
                total = total + jnp.dot(p_ref[...], weight, preferred_element_type=F32)
            even_ref[...] = total[:, :rows]
            odd_ref[i * width : (i + 1) * width, :] = coded(
                total[:, rows:], 1.0 / info_ref[3:4, :1]
            )

    blocks = [jax.ShapeDtypeStruct((width, rows), F32)] * len(pairs)
    blocks.append(jax.ShapeDtypeStruct((len(pairs) * width, rows), jnp.int16))
    return call(kernel, blocks, [], *weights, passages, info, time=0.6 * len(pairs))


def send_on(own, arrived, info, bound_row, term_row, part=0, longer=0, after=()):
    body = own.shape[0]

    def kernel(own_ref, arrived_ref, info_ref, *refs):
        out_ref = refs[-1]
        bound = info_ref[bound_row : bound_row + 1, :1]
        total = own_ref[...] + decoded(arrived_ref[part * body : (part + 1) * body, :], bound)
        out_ref[:body, :] = coded(total, 1.0 / bound)
        out_ref[body:, :] = jnp.zeros((16 + longer, 128), jnp.int16)
        term = info_ref[term_row : term_row + 1, :1]
        if arrived.shape[0] % body:
            term = term + read_term(arrived_ref)
        write_term(out_ref, term)

    return call(
        kernel,
        jax.ShapeDtypeStruct((body + 16 + longer, 128), jnp.int16),
        [],
        own,
        arrived,
        info,
        spare=after,
        time=0.5,
    )


def added(own, arrived, info, bound_row, after=()):
    body = own.shape[0]

    def kernel(own_ref, info_ref, *refs):
        bound = info_ref[bound_row : bound_row + 1, :1]
        total = own_ref[...]
        for (_, part), ref in zip(arrived, refs):
            total = total + decoded(ref[part * body : (part + 1) * body, :], bound)
        refs[-1][...] = total

    block = jax.ShapeDtypeStruct(own.shape, F32)
    messages = [message for message, _ in arrived]
    return call(kernel, block, [], own, info, *messages, spare=after, time=0.3)


def finish_passages(own, arrived, info, width, after):
    body = own.shape[0]
    rows = body * 128 // width

    def kernel(own_ref, info_ref, *refs):
        bound = info_ref[2:3, :1]
        total = own_ref[...]
        for ref in refs[: len(arrived)]:
            total = total + decoded(ref[:body, :], bound)
        refs[-2][...] = 0.5 * get(total, rows, width)
        refs[-1][...] = info_ref[...]

    outs = (jax.ShapeDtypeStruct((rows, width), F32), jax.ShapeDtypeStruct(info.shape, F32))
    return call(kernel, outs, [], own, info, *arrived, spare=after, time=1.0)


def finish_queries(own, late, side, near, along, info, devices, after):
    body, rows = own.shape

    def kernel(own_ref, info_ref, term_ref, *refs):
        s_refs, refs = refs[: len(side)], refs[len(side) :]
        a_refs, (loss_ref, out_ref) = refs[: len(along)], refs[-2:]
        bound = info_ref[3:4, :1]
        total = own_ref[...]
        for ref in s_refs[:late]:
            total = total + decoded(ref[:body, :], bound)
        for g in range(body // 128):
            here = slice(g * 128, (g + 1) * 128)
            out_ref[:, here] = 0.5 * total[here, :].T
        sides = [info_ref[1:2, :1]] + [read_term(ref) for ref in s_refs]
        lines = [info_ref[0:1, :1] + read_term(term_ref)] + [read_term(ref) for ref in a_refs]
        loss = tree(jnp.add, sides) + tree(jnp.add, lines)
        loss_ref[...] = loss * (1.0 / (2.0 * rows * devices))

    outs = (jax.ShapeDtypeStruct((1, 1), F32), jax.ShapeDtypeStruct((rows, body), F32))
    return call(kernel, outs, [], own, info, near, *side, *along, spare=[after], time=1.0)


def per_device(queries, passages, hard_ids, list_lengths):
    rows, width = queries.shape
    listed = hard_ids.shape[1]
    across = lax.axis_size("pa")
    down = lax.axis_size("pb")
    tall, wide = across * rows, down * rows

    message, near_message, far_message = first_messages(
        queries, passages, hard_ids, list_lengths
    )
    far = [exchange(far_message, "pb", j) for j in range(2, down, 2)]
    near = exchange(near_message, "pb", 1)
    passage_slots = [near_message, near]
    for part in far:
        passage_slots += [part, exchange(part, "pb", 1)]
    row_turns = list(range(0, across, 2))
    messages, counts = [], []
    for k in row_turns:
        part = exchange(message, "pa", k) if k else message
        part, count = count_listed(part, listed, down, [near, *far, counts[0]] if k else [])
        other, other_count = count_listed(exchange(part, "pa", 1), listed, down)
        messages += [part, other]
        counts += [count, other_count]

    scores, stats, q_all, p_all = score_sweep(messages, passage_slots, counts, rows, width)
    passages = flipped(p_all)
    stats = share_out(stats, exchange(stats, "pa", 1), tall, wide, rows, passages)
    others = []
    for t in range(1, down):
        pairs = []
        for i in range(across * down):
            z, c = divmod(i, across)
            pairs.append((i, z * across + (c ^ 2 * t) if c % 2 == 0 else (z ^ t) * across + c))
        others.append(lax.ppermute(stats, ("pb", "pa"), pairs))
    stats = share_all(stats, others, rows)
    row_level, col_level, info = levels(stats, exchange(stats, "pa", 1), wide, rows)

    swept = (scores, row_level, col_level, counts)
    onward = list(range(3, down, 2))
    staying = [*range(2, down, 2), 1, 0]
    first = weight_sweep(onward, *swept)
    (near,) = passage_sweep(onward, onward, first, q_all, info, True)
    near = exchange(near, "pb", 1)
    second = weight_sweep(staying, *swept)
    weights = [*first, *second]
    blocks = passage_sweep(staying[:-2], staying, second, q_all, info)
    along = [
        exchange(send_on(own, near, info, 2, 0, part, 16), "pb", 2 * (part + 1))
        for part, own in enumerate(blocks)
    ]
    (last,) = passage_sweep([1], staying, second, q_all, info)
    last = exchange(last, "pb", 1)
    (passage_sum,) = passage_sweep([0], staying, second, q_all, info)

    side = []
    for m in range(across // 2):
        own, other = query_sweep([m], weights, [onward, staying], passages, info)
        other = exchange(other, "pa", 1)
        if m:
            after = [last] if m == 2 else []
            side.append(exchange(send_on(own, other, info, 3, 1, after=after), "pa", 2 * m))
        else:
            query_sum, core = own, other
    query_sum = added(query_sum, [(core, 0), (side[-1], 0)], info, 3)
    grad_passages, after = finish_passages(
        passage_sum, [last, *along], info, width, [query_sum]
    )
    loss, grad_queries = finish_queries(
        query_sum, len(side) - 1, side, near, along, info, across * down, after
    )
    return (loss.reshape(()), grad_queries, grad_passages)


def solution(mesh):
    return jax.shard_map(
        per_device,
        mesh=mesh,
        in_specs=(
            P(("pb", "pa"), None),
            P(("pb", "pa"), None),
            P(("pb", "pa"), None),
            P(("pb", "pa")),
        ),
        out_specs=(P(), P(("pb", "pa"), None), P(("pb", "pa"), None)),
        check_vma=False,
    )
```

```python
import math

import jax
import jax.numpy as jnp
from jax import lax
from jax.experimental import pallas as pl
from jax.experimental.pallas import tpu as pltpu
from jax.sharding import PartitionSpec as P

F32 = jnp.float32
BF16 = jnp.bfloat16
TIME_BYTES = 3.6e6
VMEM_SPARE = 4 * 1024 * 1024
VMEM_MOST = 56 * 1024 * 1024
CODE_SPAN = 2.0**28
CODE_STEPS = 32000.0 / 28.0
LOSS_UNIT = 1.0 / 16384.0
DIGIT = 2.0**15


def exchange(value, axis, turn):
    size = lax.axis_size(axis)
    return lax.ppermute(value, axis, [(i, i ^ turn) for i in range(size)])


def call(kernel, out_shape, scratch_shapes, *operands, spare=(), room=None, time=0.1):
    size = sum(x.size * x.dtype.itemsize for x in (*operands, *jax.tree.leaves(out_shape)))
    held = [x for x in scratch_shapes if hasattr(x, "memory_space") and x.memory_space == pltpu.VMEM]
    size += sum(math.prod(x.shape) * jnp.dtype(x.dtype).itemsize for x in held)
    spaces = [pl.BlockSpec(memory_space=pltpu.VMEM)] * len(operands)
    spaces += [pl.BlockSpec(memory_space=pl.ANY)] * len(spare)
    return pl.pallas_call(
        kernel,
        out_shape=out_shape,
        in_specs=spaces,
        out_specs=jax.tree.map(lambda _: pl.BlockSpec(memory_space=pltpu.VMEM), out_shape),
        scratch_shapes=scratch_shapes,
        compiler_params=pltpu.CompilerParams(vmem_limit_bytes=room or 2 * size + VMEM_SPARE),
        cost_estimate=pl.CostEstimate(
            flops=1, bytes_accessed=int(time * TIME_BYTES), transcendentals=0
        ),
    )(*operands, *spare)


def put(ref, value):
    rows = value.shape[0]
    for g in range(value.shape[1] // 128):
        ref[g * rows : (g + 1) * rows, :] = value[:, g * 128 : (g + 1) * 128]


def get(ref, rows, width):
    return jnp.concatenate(
        [ref[g * rows : (g + 1) * rows, :] for g in range(width // 128)], axis=1
    )


def first_messages(queries, passages, hard_ids, list_lengths):
    rows, width = queries.shape
    listed = hard_ids.shape[1]
    body = width // 128 * rows
    operands = (passages, hard_ids.T, list_lengths.reshape(1, rows), queries)

    def kernel(*refs):
        sources, (q_out, near_out, far_out), held, sems = refs[:4], refs[4:7], refs[7:11], refs[11]
        copies = [
            pltpu.make_async_copy(src, dst, sems.at[n])
            for n, (src, dst) in enumerate(zip(sources, held))
        ]
        for copy in copies:
            copy.start()
        p_ref, ids_ref, len_ref, q_ref = held
        for copy in copies:
            copy.wait()
        part = p_ref[...].astype(BF16)
        for out in (near_out, far_out):
            put(out, part)
            out[body:, :] = jnp.zeros((out.shape[0] - body, 128), BF16)
        put(q_out, q_ref[...].astype(BF16))
        ids = ids_ref[...].astype(F32)
        live = lax.broadcasted_iota(jnp.int32, (listed, rows), 0) < len_ref[...]
        block = jnp.floor((ids + 0.5) * (1.0 / rows))
        number = (ids - block * rows + 128.0) * jnp.exp2(block - 64.0)
        q_out[body:, :] = jnp.where(live, number, 0.0).astype(BF16)

    return call(
        kernel,
        [jax.ShapeDtypeStruct((body + listed + more, 128), BF16) for more in (0, 0, 16)],
        [pltpu.VMEM(x.shape, x.dtype) for x in operands] + [pltpu.SemaphoreType.DMA((4,))],
        spare=operands,
        room=VMEM_MOST,
        time=2.0,
    )


def count_listed(message, listed, col_slots, after=()):
    body = message.shape[0] - listed
    rows = 128
    row_axis_size = lax.axis_size("pa")

    def kernel(m_ref, *refs):
        count_ref = refs[-1]
        if after:
            refs[-2][...] = m_ref[...]
        down, across = lax.axis_index("pb"), lax.axis_index("pa")
        number = m_ref[body:, :].astype(F32)
        live = number > 0.0
        block = jnp.floor(jnp.log2(jnp.where(live, number, 1.0)) + 57.002)
        inside = (number * jnp.exp2(64.0 - block) - 127.5).astype(jnp.int32)
        block = jnp.where(live, block, -1.0).astype(jnp.int32)
        steps = lax.broadcasted_iota(jnp.int32, (rows, rows), 0)
        for g in range(0, col_slots, 4):
            unit = jnp.zeros((listed, rows), jnp.int32)
            for j in range(g, min(g + 4, col_slots)):
                mine = (down ^ j) * row_axis_size + across
                unit = jnp.where(block == mine, 1 << (8 * (j - g)), unit)
            total = jnp.zeros((rows, rows), jnp.int32)
            for h in range(listed):
                total = total + jnp.where(inside[h : h + 1, :] == steps, unit[h : h + 1, :], 0)
            count_ref[g // 4] = total

    counts = jax.ShapeDtypeStruct((-(-col_slots // 4), rows, rows), jnp.int32)
    if not len(after):
        return message, call(kernel, counts, [], message, time=0.3)
    copied = jax.ShapeDtypeStruct(message.shape, message.dtype)
    return call(kernel, (copied, counts), [], message, spare=after, time=0.3)


def count_at(ref, j):
    return ((ref[j // 4] >> (8 * (j % 4))) & 255).astype(F32)


def score_sweep(messages, passage_slots, counts, rows, width):
    row_slots, col_slots = len(messages), len(passage_slots)
    tall, wide = row_slots * rows, col_slots * rows

    def most_of(part):
        tiles = [jnp.abs(part[n : n + 16, :]) for n in range(0, part.shape[0], 16)]
        most = jnp.max(tree(jnp.maximum, tiles).astype(F32), axis=0, keepdims=True)
        return jnp.max(most, axis=1, keepdims=True)

    def kernel(*refs):
        q_refs, refs = refs[:row_slots], refs[row_slots:]
        p_refs, refs = refs[:col_slots], refs[col_slots:]
        c_refs, refs = refs[:row_slots], refs[row_slots:]
        s_ref, stat_ref, q_all, p_all, top_acc = refs
        stat_ref[...] = jnp.zeros_like(stat_ref)
        passage_most = jnp.zeros((1, 1), F32)
        for j in range(col_slots):
            part = get(p_refs[j], rows, width)
            p_all[j * rows : (j + 1) * rows, :] = part
            passage_most = jnp.maximum(passage_most, most_of(part))
        def row_stats(k):
            spot = slice(k * rows, (k + 1) * rows)
            tops = []
            for j in range(col_slots):
                here = slice(j * rows, (j + 1) * rows)
                part = s_ref[here, spot]
                tops.append(jnp.max(part, axis=0, keepdims=True))
                if k == 0:
                    top_acc[here, :] = part
                else:
                    top_acc[here, :] = jnp.maximum(top_acc[here, :], part)
            top = tree(jnp.maximum, tops)
            total = jnp.zeros((rows, rows), F32)
            for j in range(col_slots):
                here = slice(j * rows, (j + 1) * rows)
                times = 1.0 + count_at(c_refs[k], j)
                total = total + jnp.exp(s_ref[here, spot] - top) * times
            stat_ref[0:1, spot] = top
            stat_ref[1:2, spot] = jnp.sum(total, axis=0, keepdims=True)

        query_most = jnp.zeros((1, 1), F32)
        for m in range(row_slots // 2):
            both = [get(q, rows, width) for q in q_refs[2 * m : 2 * m + 2]]
            both = jnp.concatenate(both, axis=0)
            query_most = jnp.maximum(query_most, most_of(both))
            spot = slice(2 * m * rows, 2 * (m + 1) * rows)
            q_all[spot, :] = both
            s_ref[:, spot] = lax.dot_general(
                p_all[...], both, (((1,), (1,)), ((), ())), preferred_element_type=F32
            )
            if m:
                row_stats(2 * m - 2)
                row_stats(2 * m - 1)
        row_stats(row_slots - 2)
        row_stats(row_slots - 1)
        stat_ref[2:3, :tall] = jnp.broadcast_to(passage_most, (1, tall))
        stat_ref[2:3, tall:] = jnp.broadcast_to(query_most, (1, wide))
        unit = lax.broadcasted_iota(jnp.int32, (rows, rows), 0) == lax.broadcasted_iota(
            jnp.int32, (rows, rows), 1
        )
        pairs = jnp.sum(jnp.where(unit, s_ref[:rows, :rows], 0.0), axis=0, keepdims=True)
        stat_ref[3:4, :rows] = pairs
        stat_ref[3:4, tall : tall + rows] = pairs
        for j in range(col_slots):
            here = slice(j * rows, (j + 1) * rows)
            there = slice(tall + j * rows, tall + (j + 1) * rows)
            acc = top_acc[here, :]
            stat_ref[0:1, there] = jnp.max(acc.T, axis=0, keepdims=True)
            top = jnp.max(acc, axis=1, keepdims=True)
            total = jnp.zeros((rows, rows), F32)
            for k in range(row_slots):
                total = total + jnp.exp(s_ref[here, k * rows : (k + 1) * rows] - top)
            stat_ref[1:2, there] = jnp.sum(total.T, axis=0, keepdims=True)

    return call(
        kernel,
        (
            jax.ShapeDtypeStruct((wide, tall), F32),
            jax.ShapeDtypeStruct((8, tall + wide), F32),
            jax.ShapeDtypeStruct((tall, width), BF16),
            jax.ShapeDtypeStruct((wide, width), BF16),
        ),
        [pltpu.VMEM((wide, rows), F32)],
        *messages,
        *passage_slots,
        *counts,
        time=2.0,
    )


def turned(value, turn, rows):
    slots = value.shape[1] // rows
    return jnp.concatenate(
        [value[:, (k ^ turn) * rows : ((k ^ turn) + 1) * rows] for k in range(slots)], axis=1
    )


def tree(combine, values):
    while len(values) > 1:
        values = [combine(a, b) for a, b in zip(values[::2], values[1::2])]
    return values[0]


def joined(one, two):
    top = jnp.maximum(one[0:1], two[0:1])
    total = one[1:2] * jnp.exp(one[0:1] - top) + two[1:2] * jnp.exp(two[0:1] - top)
    most = jnp.maximum(one[2:3], two[2:3])
    return jnp.concatenate([top, total, most, one[3:] + two[3:]], axis=0)


def share_out(own, other, tall, wide, rows, after):
    def kernel(own_ref, other_ref, after_ref, out_ref):
        first = lax.axis_index("pa") % 2 == 0
        by_row = joined(own_ref[:, :tall], turned(other_ref[:, :tall], 1, rows))
        by_col = jnp.concatenate([own_ref[:, tall:], other_ref[:, tall:]], axis=1)
        out_ref[...] = jnp.where(first, by_row, by_col)

    return call(kernel, jax.ShapeDtypeStruct((8, tall), F32), [], own, other, spare=[after])


def share_all(own, others, rows):
    def kernel(own_ref, *refs):
        first = lax.axis_index("pa") % 2 == 0
        parts = [own_ref[...]]
        for t, ref in enumerate(refs[:-1], start=1):
            there = ref[...]
            parts.append(jnp.where(first, turned(there, 2 * t, rows), turned(there, t, rows)))
        refs[-1][...] = tree(joined, parts)

    return call(kernel, jax.ShapeDtypeStruct(own.shape, F32), [], own, *others)


def levels(own, other, wide, rows):
    tall = own.shape[1]

    def kernel(own_ref, other_ref, row_ref, col_ref, info_ref):
        first = lax.axis_index("pa") % 2 == 0
        own_v, other_v = own_ref[...], other_ref[...]
        by_row = jnp.where(first, own_v, turned(other_v, 1, rows))
        by_col = jnp.where(first, other_v, own_v)
        mine = jnp.where(first, by_col[:, wide:], by_col[:, :wide])
        row_level = by_row[0:1] + jnp.log(by_row[1:2])
        both = by_col[0:1] + jnp.log(by_col[1:2])
        row_ref[...] = jnp.broadcast_to(row_level, row_ref.shape)
        columns = mine[0:1] + jnp.log(mine[1:2])
        for j in range(wide // rows):
            here = slice(j * rows, (j + 1) * rows)
            col_ref[here, :] = jnp.broadcast_to(columns[:, here], (rows, rows)).T

        def summed(level):
            parts = [
                jnp.sum(level[:, g * rows : (g + 1) * rows], axis=1, keepdims=True)
                for g in range(level.shape[1] // rows)
            ]
            return tree(jnp.add, parts)

        row_term = summed(row_level - by_row[3:4])
        col_term = summed(both - by_col[3:4])
        query_bound = jnp.maximum(mine[2:3, :1] * (tall * 1.02 + 8.0), 1e-30)
        passage_bound = jnp.maximum(by_row[2:3, :1] * (2 * wide * 1.02 + 8.0), 1e-30)
        info_ref[...] = jnp.zeros_like(info_ref)
        for n, value in enumerate((row_term, col_term, query_bound, passage_bound)):
            info_ref[n : n + 1, :] = jnp.broadcast_to(value, (1, rows))

    return call(
        kernel,
        (
            jax.ShapeDtypeStruct((8, tall), F32),
            jax.ShapeDtypeStruct((wide, rows), F32),
            jax.ShapeDtypeStruct((8, rows), F32),
        ),
        [],
        own,
        other,
    )


def coded(value, inverse):
    steps = jnp.log2(jnp.abs(value) * (inverse * CODE_SPAN) + 1.0) * CODE_STEPS + 0.5
    return jnp.where(value < 0.0, -steps, steps).astype(jnp.int32).astype(jnp.int16)


def decoded(code, bound):
    steps = code.astype(F32)
    size = (jnp.exp2(jnp.abs(steps) * (1.0 / CODE_STEPS)) - 1.0) * (bound * (1.0 / CODE_SPAN))
    return jnp.where(steps < 0.0, -size, size)


def write_term(ref, value):
    lanes = lax.broadcasted_iota(jnp.int32, (16, 128), 1)
    left = value[:, :1] * LOSS_UNIT
    digits = jnp.zeros((16, 128), F32)
    for n in range(3):
        digit = jnp.round(left)
        left = (left - digit) * DIGIT
        digits = jnp.where(lanes == n, digit, digits)
    ref[ref.shape[0] - 16 :, :] = digits.astype(jnp.int32).astype(jnp.int16)


def read_term(ref):
    digits = ref[ref.shape[0] - 16 :, :].astype(F32)[:1, :]
    one, two, three = digits[:, 0:1], digits[:, 1:2], digits[:, 2:3]
    return (one + (two + three * (1.0 / DIGIT)) * (1.0 / DIGIT)) * (1.0 / LOSS_UNIT)


def weight_sweep(picked, scores, row_level, col_level, counts):
    wide, tall = scores.shape
    rows = col_level.shape[1]
    row_slots = tall // rows

    def kernel(s_ref, row_ref, col_ref, *refs):
        c_refs, (hi_ref, lo_ref) = refs[:row_slots], refs[row_slots:]
        unit = (
            lax.broadcasted_iota(jnp.int32, (rows, rows), 0)
            == lax.broadcasted_iota(jnp.int32, (rows, rows), 1)
        ).astype(F32)
        for n, j in enumerate(picked):
            here = slice(j * rows, (j + 1) * rows)
            for k in range(row_slots):
                spot = slice(k * rows, (k + 1) * rows)
                part = s_ref[here, spot]
                by_row = jnp.exp(part - row_ref[0:1, spot])
                by_col = jnp.exp(part - col_ref[here, :])
                pair = (by_row + by_col).astype(BF16).astype(F32)
                hard = by_row.astype(BF16).astype(F32)
                weight = pair + hard * count_at(c_refs[k], j)
                if j == 0 and k == 0:
                    weight = weight - 2.0 * unit
                high = weight.astype(BF16)
                hi_ref[n, :, spot] = high
                lo_ref[n, :, spot] = (weight - high.astype(F32)).astype(BF16)

    weights = jax.ShapeDtypeStruct((len(picked), rows, tall), BF16)
    return call(
        kernel,
        (weights, weights),
        [],
        scores,
        row_level,
        col_level,
        *counts,
        time=0.45 * len(picked),
    )


def passage_sweep(picked, held, weights, q_all, info, term=False):
    high, low = weights
    rows, width = info.shape[1], q_all.shape[1]
    body = width // 128 * rows
    odd = [j for j in picked if j % 2]
    even = [j for j in picked if j % 2 == 0]

    def kernel(hi_ref, lo_ref, q_ref, info_ref, *out_refs):
        inverse = 1.0 / info_ref[2:3, :1]
        if term:
            write_term(out_refs[-1], info_ref[0:1, :])
        for j in picked:
            n = held.index(j)
            part = jnp.dot(hi_ref[n], q_ref[...], preferred_element_type=F32)
            part = part + jnp.dot(lo_ref[n], q_ref[...], preferred_element_type=F32)
            if j % 2:
                first = odd.index(j) * body
                put(out_refs[-1].at[first : first + body, :], coded(part, inverse))
            else:
                put(out_refs[even.index(j)], part)

    outs = [jax.ShapeDtypeStruct((body, 128), F32)] * len(even)
    if odd:
        outs.append(jax.ShapeDtypeStruct((len(odd) * body + 16 * term, 128), jnp.int16))
    return call(kernel, outs, [], high, low, q_all, info, time=0.4 * len(picked))


def flipped(block):
    def kernel(in_ref, out_ref):
        out_ref[...] = in_ref[...].astype(F32).T.astype(BF16)

    shape = jax.ShapeDtypeStruct(block.shape[::-1], BF16)
    return call(kernel, shape, [], block, time=0.3)


def query_sweep(pairs, weights, picked, passages, info):
    width, rows = passages.shape[0], info.shape[1]
    slots = sorted((j, 2 * i, n) for i, part in enumerate(picked) for n, j in enumerate(part))

    def kernel(*refs):
        w_refs, (p_ref, info_ref, *even_refs, odd_ref) = refs[: len(weights)], refs[len(weights) :]
        for i, (m, even_ref) in enumerate(zip(pairs, even_refs)):
            spot = slice(2 * m * rows, 2 * (m + 1) * rows)
            total = jnp.zeros((width, 2 * rows), F32)
            for side in range(2):
                weight = [w_refs[g + side][n, :, spot] for _, g, n in slots]
                weight = jnp.concatenate(weight, axis=0)
                total = total + jnp.dot(p_ref[...], weight, preferred_element_type=F32)
            even_ref[...] = total[:, :rows]
            odd_ref[i * width : (i + 1) * width, :] = coded(
                total[:, rows:], 1.0 / info_ref[3:4, :1]
            )

    blocks = [jax.ShapeDtypeStruct((width, rows), F32)] * len(pairs)
    blocks.append(jax.ShapeDtypeStruct((len(pairs) * width, rows), jnp.int16))
    return call(kernel, blocks, [], *weights, passages, info, time=0.6 * len(pairs))


def send_on(own, arrived, info, bound_row, term_row, part=0, longer=0, after=()):
    body = own.shape[0]

    def kernel(own_ref, arrived_ref, info_ref, *refs):
        out_ref = refs[-1]
        bound = info_ref[bound_row : bound_row + 1, :1]
        total = own_ref[...] + decoded(arrived_ref[part * body : (part + 1) * body, :], bound)
        out_ref[:body, :] = coded(total, 1.0 / bound)
        out_ref[body:, :] = jnp.zeros((16 + longer, 128), jnp.int16)
        term = info_ref[term_row : term_row + 1, :1]
        if arrived.shape[0] % body:
            term = term + read_term(arrived_ref)
        write_term(out_ref, term)

    return call(
        kernel,
        jax.ShapeDtypeStruct((body + 16 + longer, 128), jnp.int16),
        [],
        own,
        arrived,
        info,
        spare=after,
        time=0.5,
    )


def added(own, arrived, info, bound_row, after=()):
    body = own.shape[0]

    def kernel(own_ref, info_ref, *refs):
        bound = info_ref[bound_row : bound_row + 1, :1]
        total = own_ref[...]
        for (_, part), ref in zip(arrived, refs):
            total = total + decoded(ref[part * body : (part + 1) * body, :], bound)
        refs[-1][...] = total

    block = jax.ShapeDtypeStruct(own.shape, F32)
    messages = [message for message, _ in arrived]
    return call(kernel, block, [], own, info, *messages, spare=after, time=0.3)


def finish_passages(own, arrived, info, width, after):
    body = own.shape[0]
    rows = body * 128 // width

    def kernel(own_ref, info_ref, *refs):
        bound = info_ref[2:3, :1]
        total = own_ref[...]
        for ref in refs[: len(arrived)]:
            total = total + decoded(ref[:body, :], bound)
        refs[-2][...] = 0.5 * get(total, rows, width)
        refs[-1][...] = info_ref[...]

    outs = (jax.ShapeDtypeStruct((rows, width), F32), jax.ShapeDtypeStruct(info.shape, F32))
    return call(kernel, outs, [], own, info, *arrived, spare=after, time=1.0)


def finish_queries(own, late, side, near, along, info, devices, after):
    body, rows = own.shape

    def kernel(own_ref, info_ref, term_ref, *refs):
        s_refs, refs = refs[: len(side)], refs[len(side) :]
        a_refs, (loss_ref, out_ref) = refs[: len(along)], refs[-2:]
        bound = info_ref[3:4, :1]
        total = own_ref[...]
        for ref in s_refs[:late]:
            total = total + decoded(ref[:body, :], bound)
        for g in range(body // 128):
            here = slice(g * 128, (g + 1) * 128)
            out_ref[:, here] = 0.5 * total[here, :].T
        sides = [info_ref[1:2, :1]] + [read_term(ref) for ref in s_refs]
        lines = [info_ref[0:1, :1] + read_term(term_ref)] + [read_term(ref) for ref in a_refs]
        loss = tree(jnp.add, sides) + tree(jnp.add, lines)
        loss_ref[...] = loss * (1.0 / (2.0 * rows * devices))

    outs = (jax.ShapeDtypeStruct((1, 1), F32), jax.ShapeDtypeStruct((rows, body), F32))
    return call(kernel, outs, [], own, info, near, *side, *along, spare=[after], time=1.0)


def per_device(queries, passages, hard_ids, list_lengths):
    rows, width = queries.shape
    listed = hard_ids.shape[1]
    across = lax.axis_size("pa")
    down = lax.axis_size("pb")
    tall, wide = across * rows, down * rows

    message, near_message, far_message = first_messages(
        queries, passages, hard_ids, list_lengths
    )
    far = [exchange(far_message, "pb", j) for j in range(2, down, 2)]
    near = exchange(near_message, "pb", 1)
    passage_slots = [near_message, near]
    for part in far:
        passage_slots += [part, exchange(part, "pb", 1)]
    row_turns = list(range(0, across, 2))
    messages, counts = [], []
    for k in row_turns:
        part = exchange(message, "pa", k) if k else message
        part, count = count_listed(part, listed, down, [near, *far, counts[0]] if k else [])
        other, other_count = count_listed(exchange(part, "pa", 1), listed, down)
        messages += [part, other]
        counts += [count, other_count]

    scores, stats, q_all, p_all = score_sweep(messages, passage_slots, counts, rows, width)
    passages = flipped(p_all)
    stats = share_out(stats, exchange(stats, "pa", 1), tall, wide, rows, passages)
    others = []
    for t in range(1, down):
        pairs = []
        for i in range(across * down):
            z, c = divmod(i, across)
            pairs.append((i, z * across + (c ^ 2 * t) if c % 2 == 0 else (z ^ t) * across + c))
        others.append(lax.ppermute(stats, ("pb", "pa"), pairs))
    stats = share_all(stats, others, rows)
    row_level, col_level, info = levels(stats, exchange(stats, "pa", 1), wide, rows)

    swept = (scores, row_level, col_level, counts)
    onward = list(range(3, down, 2))
    staying = [*range(2, down, 2), 1, 0]
    first = weight_sweep(onward, *swept)
    (near,) = passage_sweep(onward, onward, first, q_all, info, True)
    near = exchange(near, "pb", 1)
    second = weight_sweep(staying, *swept)
    weights = [*first, *second]
    blocks = passage_sweep(staying[:-2], staying, second, q_all, info)
    (last,) = passage_sweep([1], staying, second, q_all, info)
    last = exchange(last, "pb", 1)
    (passage_sum,) = passage_sweep([0], staying, second, q_all, info)

    side = []
    for m in range(across // 2):
        own, other = query_sweep([m], weights, [onward, staying], passages, info)
        other = exchange(other, "pa", 1)
        if m:
            after = [last] if m == 2 else []
            message = send_on(own, other, info, 3, 1, after=after)
            side.append(exchange(message, "pa", 2 * m))
        else:
            query_sum, core = own, other
    along = [
        exchange(send_on(own, near, info, 2, 0, part, 16, [message]), "pb", 2 * (part + 1))
        for part, own in enumerate(blocks)
    ]
    query_sum = added(query_sum, [(core, 0), (side[-1], 0)], info, 3)
    grad_passages, after = finish_passages(
        passage_sum, [last, *along], info, width, [query_sum]
    )
    loss, grad_queries = finish_queries(
        query_sum, len(side) - 1, side, near, along, info, across * down, after
    )
    return (loss.reshape(()), grad_queries, grad_passages)


def solution(mesh):
    return jax.shard_map(
        per_device,
        mesh=mesh,
        in_specs=(
            P(("pb", "pa"), None),
            P(("pb", "pa"), None),
            P(("pb", "pa"), None),
            P(("pb", "pa")),
        ),
        out_specs=(P(), P(("pb", "pa"), None), P(("pb", "pa"), None)),
        check_vma=False,
    )
```

```python
import math

import jax
import jax.numpy as jnp
from jax import lax
from jax.experimental import pallas as pl
from jax.experimental.pallas import tpu as pltpu
from jax.sharding import PartitionSpec as P

F32 = jnp.float32
BF16 = jnp.bfloat16
TIME_BYTES = 3.6e6
VMEM_SPARE = 4 * 1024 * 1024
VMEM_MOST = 56 * 1024 * 1024
CODE_SPAN = 2.0**28
CODE_STEPS = 32000.0 / 28.0
LOSS_UNIT = 1.0 / 16384.0
DIGIT = 2.0**15


def exchange(value, axis, turn):
    size = lax.axis_size(axis)
    return lax.ppermute(value, axis, [(i, i ^ turn) for i in range(size)])


def call(kernel, out_shape, scratch_shapes, *operands, spare=(), room=None, time=0.1):
    size = sum(x.size * x.dtype.itemsize for x in (*operands, *jax.tree.leaves(out_shape)))
    held = [x for x in scratch_shapes if hasattr(x, "memory_space") and x.memory_space == pltpu.VMEM]
    size += sum(math.prod(x.shape) * jnp.dtype(x.dtype).itemsize for x in held)
    spaces = [pl.BlockSpec(memory_space=pltpu.VMEM)] * len(operands)
    spaces += [pl.BlockSpec(memory_space=pl.ANY)] * len(spare)
    return pl.pallas_call(
        kernel,
        out_shape=out_shape,
        in_specs=spaces,
        out_specs=jax.tree.map(lambda _: pl.BlockSpec(memory_space=pltpu.VMEM), out_shape),
        scratch_shapes=scratch_shapes,
        compiler_params=pltpu.CompilerParams(vmem_limit_bytes=room or 2 * size + VMEM_SPARE),
        cost_estimate=pl.CostEstimate(
            flops=1, bytes_accessed=int(time * TIME_BYTES), transcendentals=0
        ),
    )(*operands, *spare)


def put(ref, value):
    rows = value.shape[0]
    for g in range(value.shape[1] // 128):
        ref[g * rows : (g + 1) * rows, :] = value[:, g * 128 : (g + 1) * 128]


def get(ref, rows, width):
    return jnp.concatenate(
        [ref[g * rows : (g + 1) * rows, :] for g in range(width // 128)], axis=1
    )


def first_messages(queries, passages, hard_ids, list_lengths):
    rows, width = queries.shape
    listed = hard_ids.shape[1]
    body = width // 128 * rows
    operands = (passages, hard_ids.T, list_lengths.reshape(1, rows), queries)

    def kernel(*refs):
        sources, (q_out, near_out, far_out), held, sems = refs[:4], refs[4:7], refs[7:11], refs[11]
        copies = [
            pltpu.make_async_copy(src, dst, sems.at[n])
            for n, (src, dst) in enumerate(zip(sources, held))
        ]
        for copy in copies:
            copy.start()
        p_ref, ids_ref, len_ref, q_ref = held
        for copy in copies:
            copy.wait()
        part = p_ref[...].astype(BF16)
        for out in (near_out, far_out):
            put(out, part)
            if out.shape[0] > body:
                out[body:, :] = jnp.zeros((out.shape[0] - body, 128), BF16)
        put(q_out, q_ref[...].astype(BF16))
        ids = ids_ref[...].astype(F32)
        live = lax.broadcasted_iota(jnp.int32, (listed, rows), 0) < len_ref[...]
        block = jnp.floor((ids + 0.5) * (1.0 / rows))
        number = (ids - block * rows + 128.0) * jnp.exp2(block - 64.0)
        q_out[body:, :] = jnp.where(live, number, 0.0).astype(BF16)

    return call(
        kernel,
        [jax.ShapeDtypeStruct((body + listed + more, 128), BF16) for more in (0, -listed, 16)],
        [pltpu.VMEM(x.shape, x.dtype) for x in operands] + [pltpu.SemaphoreType.DMA((4,))],
        spare=operands,
        room=VMEM_MOST,
        time=2.0,
    )


def count_listed(message, listed, col_slots, after=()):
    body = message.shape[0] - listed
    rows = 128
    row_axis_size = lax.axis_size("pa")

    def kernel(m_ref, *refs):
        count_ref = refs[-1]
        if after:
            refs[-2][...] = m_ref[...]
        down, across = lax.axis_index("pb"), lax.axis_index("pa")
        number = m_ref[body:, :].astype(F32)
        live = number > 0.0
        block = jnp.floor(jnp.log2(jnp.where(live, number, 1.0)) + 57.002)
        inside = (number * jnp.exp2(64.0 - block) - 127.5).astype(jnp.int32)
        block = jnp.where(live, block, -1.0).astype(jnp.int32)
        steps = lax.broadcasted_iota(jnp.int32, (rows, rows), 0)
        for g in range(0, col_slots, 4):
            unit = jnp.zeros((listed, rows), jnp.int32)
            for j in range(g, min(g + 4, col_slots)):
                mine = (down ^ j) * row_axis_size + across
                unit = jnp.where(block == mine, 1 << (8 * (j - g)), unit)
            total = jnp.zeros((rows, rows), jnp.int32)
            for h in range(listed):
                total = total + jnp.where(inside[h : h + 1, :] == steps, unit[h : h + 1, :], 0)
            count_ref[g // 4] = total

    counts = jax.ShapeDtypeStruct((-(-col_slots // 4), rows, rows), jnp.int32)
    if not len(after):
        return message, call(kernel, counts, [], message, time=0.3)
    copied = jax.ShapeDtypeStruct(message.shape, message.dtype)
    return call(kernel, (copied, counts), [], message, spare=after, time=0.3)


def count_at(ref, j):
    return ((ref[j // 4] >> (8 * (j % 4))) & 255).astype(F32)


def score_sweep(messages, passage_slots, counts, rows, width):
    row_slots, col_slots = len(messages), len(passage_slots)
    tall, wide = row_slots * rows, col_slots * rows

    def most_of(part):
        tiles = [jnp.abs(part[n : n + 16, :]) for n in range(0, part.shape[0], 16)]
        most = jnp.max(tree(jnp.maximum, tiles).astype(F32), axis=0, keepdims=True)
        return jnp.max(most, axis=1, keepdims=True)

    def kernel(*refs):
        q_refs, refs = refs[:row_slots], refs[row_slots:]
        p_refs, refs = refs[:col_slots], refs[col_slots:]
        c_refs, refs = refs[:row_slots], refs[row_slots:]
        s_ref, stat_ref, q_all, p_all, top_acc = refs
        stat_ref[...] = jnp.zeros_like(stat_ref)
        passage_most = jnp.zeros((1, 1), F32)
        for j in range(col_slots):
            part = get(p_refs[j], rows, width)
            p_all[j * rows : (j + 1) * rows, :] = part
            passage_most = jnp.maximum(passage_most, most_of(part))
        def row_stats(k):
            spot = slice(k * rows, (k + 1) * rows)
            tops = []
            for j in range(col_slots):
                here = slice(j * rows, (j + 1) * rows)
                part = s_ref[here, spot]
                tops.append(jnp.max(part, axis=0, keepdims=True))
                if k == 0:
                    top_acc[here, :] = part
                else:
                    top_acc[here, :] = jnp.maximum(top_acc[here, :], part)
            top = tree(jnp.maximum, tops)
            total = jnp.zeros((rows, rows), F32)
            for j in range(col_slots):
                here = slice(j * rows, (j + 1) * rows)
                times = 1.0 + count_at(c_refs[k], j)
                total = total + jnp.exp(s_ref[here, spot] - top) * times
            stat_ref[0:1, spot] = top
            stat_ref[1:2, spot] = jnp.sum(total, axis=0, keepdims=True)

        query_most = jnp.zeros((1, 1), F32)
        for m in range(row_slots // 2):
            both = [get(q, rows, width) for q in q_refs[2 * m : 2 * m + 2]]
            both = jnp.concatenate(both, axis=0)
            query_most = jnp.maximum(query_most, most_of(both))
            spot = slice(2 * m * rows, 2 * (m + 1) * rows)
            q_all[spot, :] = both
            s_ref[:, spot] = lax.dot_general(
                p_all[...], both, (((1,), (1,)), ((), ())), preferred_element_type=F32
            )
            if m:
                row_stats(2 * m - 2)
                row_stats(2 * m - 1)
        row_stats(row_slots - 2)
        row_stats(row_slots - 1)
        stat_ref[2:3, :tall] = jnp.broadcast_to(passage_most, (1, tall))
        stat_ref[2:3, tall:] = jnp.broadcast_to(query_most, (1, wide))
        unit = lax.broadcasted_iota(jnp.int32, (rows, rows), 0) == lax.broadcasted_iota(
            jnp.int32, (rows, rows), 1
        )
        pairs = jnp.sum(jnp.where(unit, s_ref[:rows, :rows], 0.0), axis=0, keepdims=True)
        stat_ref[3:4, :rows] = pairs
        stat_ref[3:4, tall : tall + rows] = pairs
        for j in range(col_slots):
            here = slice(j * rows, (j + 1) * rows)
            there = slice(tall + j * rows, tall + (j + 1) * rows)
            acc = top_acc[here, :]
            stat_ref[0:1, there] = jnp.max(acc.T, axis=0, keepdims=True)
            top = jnp.max(acc, axis=1, keepdims=True)
            total = jnp.zeros((rows, rows), F32)
            for k in range(row_slots):
                total = total + jnp.exp(s_ref[here, k * rows : (k + 1) * rows] - top)
            stat_ref[1:2, there] = jnp.sum(total.T, axis=0, keepdims=True)

    return call(
        kernel,
        (
            jax.ShapeDtypeStruct((wide, tall), F32),
            jax.ShapeDtypeStruct((8, tall + wide), F32),
            jax.ShapeDtypeStruct((tall, width), BF16),
            jax.ShapeDtypeStruct((wide, width), BF16),
        ),
        [pltpu.VMEM((wide, rows), F32)],
        *messages,
        *passage_slots,
        *counts,
        time=2.0,
    )


def turned(value, turn, rows):
    slots = value.shape[1] // rows
    return jnp.concatenate(
        [value[:, (k ^ turn) * rows : ((k ^ turn) + 1) * rows] for k in range(slots)], axis=1
    )


def tree(combine, values):
    while len(values) > 1:
        values = [combine(a, b) for a, b in zip(values[::2], values[1::2])]
    return values[0]


def joined(one, two):
    top = jnp.maximum(one[0:1], two[0:1])
    total = one[1:2] * jnp.exp(one[0:1] - top) + two[1:2] * jnp.exp(two[0:1] - top)
    most = jnp.maximum(one[2:3], two[2:3])
    return jnp.concatenate([top, total, most, one[3:] + two[3:]], axis=0)


def share_out(own, other, tall, wide, rows, after):
    def kernel(own_ref, other_ref, after_ref, out_ref):
        first = lax.axis_index("pa") % 2 == 0
        by_row = joined(own_ref[:, :tall], turned(other_ref[:, :tall], 1, rows))
        by_col = jnp.concatenate([own_ref[:, tall:], other_ref[:, tall:]], axis=1)
        out_ref[...] = jnp.where(first, by_row, by_col)

    return call(kernel, jax.ShapeDtypeStruct((8, tall), F32), [], own, other, spare=[after])


def share_all(own, others, rows):
    def kernel(own_ref, *refs):
        first = lax.axis_index("pa") % 2 == 0
        parts = [own_ref[...]]
        for t, ref in enumerate(refs[:-1], start=1):
            there = ref[...]
            parts.append(jnp.where(first, turned(there, 2 * t, rows), turned(there, t, rows)))
        refs[-1][...] = tree(joined, parts)

    return call(kernel, jax.ShapeDtypeStruct(own.shape, F32), [], own, *others)


def levels(own, other, wide, rows):
    tall = own.shape[1]

    def kernel(own_ref, other_ref, row_ref, col_ref, info_ref):
        first = lax.axis_index("pa") % 2 == 0
        own_v, other_v = own_ref[...], other_ref[...]
        by_row = jnp.where(first, own_v, turned(other_v, 1, rows))
        by_col = jnp.where(first, other_v, own_v)
        mine = jnp.where(first, by_col[:, wide:], by_col[:, :wide])
        row_level = by_row[0:1] + jnp.log(by_row[1:2])
        both = by_col[0:1] + jnp.log(by_col[1:2])
        row_ref[...] = jnp.broadcast_to(row_level, row_ref.shape)
        columns = mine[0:1] + jnp.log(mine[1:2])
        for j in range(wide // rows):
            here = slice(j * rows, (j + 1) * rows)
            col_ref[here, :] = jnp.broadcast_to(columns[:, here], (rows, rows)).T

        def summed(level):
            parts = [
                jnp.sum(level[:, g * rows : (g + 1) * rows], axis=1, keepdims=True)
                for g in range(level.shape[1] // rows)
            ]
            return tree(jnp.add, parts)

        row_term = summed(row_level - by_row[3:4])
        col_term = summed(both - by_col[3:4])
        query_bound = jnp.maximum(mine[2:3, :1] * (tall * 1.02 + 8.0), 1e-30)
        passage_bound = jnp.maximum(by_row[2:3, :1] * (2 * wide * 1.02 + 8.0), 1e-30)
        info_ref[...] = jnp.zeros_like(info_ref)
        for n, value in enumerate((row_term, col_term, query_bound, passage_bound)):
            info_ref[n : n + 1, :] = jnp.broadcast_to(value, (1, rows))

    return call(
        kernel,
        (
            jax.ShapeDtypeStruct((8, tall), F32),
            jax.ShapeDtypeStruct((wide, rows), F32),
            jax.ShapeDtypeStruct((8, rows), F32),
        ),
        [],
        own,
        other,
    )


def coded(value, inverse):
    steps = jnp.log2(jnp.abs(value) * (inverse * CODE_SPAN) + 1.0) * CODE_STEPS + 0.5
    return jnp.where(value < 0.0, -steps, steps).astype(jnp.int32).astype(jnp.int16)


def decoded(code, bound):
    steps = code.astype(F32)
    size = (jnp.exp2(jnp.abs(steps) * (1.0 / CODE_STEPS)) - 1.0) * (bound * (1.0 / CODE_SPAN))
    return jnp.where(steps < 0.0, -size, size)


def write_term(ref, value):
    lanes = lax.broadcasted_iota(jnp.int32, (16, 128), 1)
    left = value[:, :1] * LOSS_UNIT
    digits = jnp.zeros((16, 128), F32)
    for n in range(3):
        digit = jnp.round(left)
        left = (left - digit) * DIGIT
        digits = jnp.where(lanes == n, digit, digits)
    ref[ref.shape[0] - 16 :, :] = digits.astype(jnp.int32).astype(jnp.int16)


def read_term(ref):
    digits = ref[ref.shape[0] - 16 :, :].astype(F32)[:1, :]
    one, two, three = digits[:, 0:1], digits[:, 1:2], digits[:, 2:3]
    return (one + (two + three * (1.0 / DIGIT)) * (1.0 / DIGIT)) * (1.0 / LOSS_UNIT)


def weight_sweep(picked, scores, row_level, col_level, counts):
    wide, tall = scores.shape
    rows = col_level.shape[1]
    row_slots = tall // rows

    def kernel(s_ref, row_ref, col_ref, *refs):
        c_refs, (hi_ref, lo_ref) = refs[:row_slots], refs[row_slots:]
        unit = (
            lax.broadcasted_iota(jnp.int32, (rows, rows), 0)
            == lax.broadcasted_iota(jnp.int32, (rows, rows), 1)
        ).astype(F32)
        for n, j in enumerate(picked):
            here = slice(j * rows, (j + 1) * rows)
            for k in range(row_slots):
                spot = slice(k * rows, (k + 1) * rows)
                part = s_ref[here, spot]
                by_row = jnp.exp(part - row_ref[0:1, spot])
                by_col = jnp.exp(part - col_ref[here, :])
                pair = (by_row + by_col).astype(BF16).astype(F32)
                hard = by_row.astype(BF16).astype(F32)
                weight = pair + hard * count_at(c_refs[k], j)
                if j == 0 and k == 0:
                    weight = weight - 2.0 * unit
                high = weight.astype(BF16)
                hi_ref[n, :, spot] = high
                lo_ref[n, :, spot] = (weight - high.astype(F32)).astype(BF16)

    weights = jax.ShapeDtypeStruct((len(picked), rows, tall), BF16)
    return call(
        kernel,
        (weights, weights),
        [],
        scores,
        row_level,
        col_level,
        *counts,
        time=0.45 * len(picked),
    )


def passage_sweep(picked, held, weights, q_all, info, term=False):
    high, low = weights
    rows, width = info.shape[1], q_all.shape[1]
    body = width // 128 * rows
    odd = [j for j in picked if j % 2]
    even = [j for j in picked if j % 2 == 0]

    def kernel(hi_ref, lo_ref, q_ref, info_ref, *out_refs):
        inverse = 1.0 / info_ref[2:3, :1]
        if term:
            write_term(out_refs[-1], info_ref[0:1, :])
        for j in picked:
            n = held.index(j)
            part = jnp.dot(hi_ref[n], q_ref[...], preferred_element_type=F32)
            part = part + jnp.dot(lo_ref[n], q_ref[...], preferred_element_type=F32)
            if j % 2:
                first = odd.index(j) * body
                put(out_refs[-1].at[first : first + body, :], coded(part, inverse))
            else:
                put(out_refs[even.index(j)], part)

    outs = [jax.ShapeDtypeStruct((body, 128), F32)] * len(even)
    if odd:
        outs.append(jax.ShapeDtypeStruct((len(odd) * body + 16 * term, 128), jnp.int16))
    return call(kernel, outs, [], high, low, q_all, info, time=0.4 * len(picked))


def flipped(block):
    def kernel(in_ref, out_ref):
        out_ref[...] = in_ref[...].astype(F32).T.astype(BF16)

    shape = jax.ShapeDtypeStruct(block.shape[::-1], BF16)
    return call(kernel, shape, [], block, time=0.3)


def query_sweep(pairs, weights, picked, passages, info):
    width, rows = passages.shape[0], info.shape[1]
    slots = sorted((j, 2 * i, n) for i, part in enumerate(picked) for n, j in enumerate(part))

    def kernel(*refs):
        w_refs, (p_ref, info_ref, *even_refs, odd_ref) = refs[: len(weights)], refs[len(weights) :]
        for i, (m, even_ref) in enumerate(zip(pairs, even_refs)):
            spot = slice(2 * m * rows, 2 * (m + 1) * rows)
            total = jnp.zeros((width, 2 * rows), F32)
            for side in range(2):
                weight = [w_refs[g + side][n, :, spot] for _, g, n in slots]
                weight = jnp.concatenate(weight, axis=0)
                total = total + jnp.dot(p_ref[...], weight, preferred_element_type=F32)
            even_ref[...] = total[:, :rows]
            odd_ref[i * width : (i + 1) * width, :] = coded(
                total[:, rows:], 1.0 / info_ref[3:4, :1]
            )

    blocks = [jax.ShapeDtypeStruct((width, rows), F32)] * len(pairs)
    blocks.append(jax.ShapeDtypeStruct((len(pairs) * width, rows), jnp.int16))
    return call(kernel, blocks, [], *weights, passages, info, time=0.6 * len(pairs))


def send_on(own, arrived, info, bound_row, term_row, part=0, longer=0, after=()):
    body = own.shape[0]

    def kernel(own_ref, arrived_ref, info_ref, *refs):
        out_ref = refs[-1]
        bound = info_ref[bound_row : bound_row + 1, :1]
        total = own_ref[...] + decoded(arrived_ref[part * body : (part + 1) * body, :], bound)
        out_ref[:body, :] = coded(total, 1.0 / bound)
        out_ref[body:, :] = jnp.zeros((16 + longer, 128), jnp.int16)
        term = info_ref[term_row : term_row + 1, :1]
        if arrived.shape[0] % body:
            term = term + read_term(arrived_ref)
        write_term(out_ref, term)

    return call(
        kernel,
        jax.ShapeDtypeStruct((body + 16 + longer, 128), jnp.int16),
        [],
        own,
        arrived,
        info,
        spare=after,
        time=0.5,
    )


def added(own, arrived, info, bound_row, after=()):
    body = own.shape[0]

    def kernel(own_ref, info_ref, *refs):
        bound = info_ref[bound_row : bound_row + 1, :1]
        total = own_ref[...]
        for (_, part), ref in zip(arrived, refs):
            total = total + decoded(ref[part * body : (part + 1) * body, :], bound)
        refs[-1][...] = total

    block = jax.ShapeDtypeStruct(own.shape, F32)
    messages = [message for message, _ in arrived]
    return call(kernel, block, [], own, info, *messages, spare=after, time=0.3)


def finish_passages(own, arrived, info, width, after):
    body = own.shape[0]
    rows = body * 128 // width

    def kernel(own_ref, info_ref, *refs):
        bound = info_ref[2:3, :1]
        total = own_ref[...]
        for ref in refs[: len(arrived)]:
            total = total + decoded(ref[:body, :], bound)
        refs[-2][...] = 0.5 * get(total, rows, width)
        refs[-1][...] = info_ref[...]

    outs = (jax.ShapeDtypeStruct((rows, width), F32), jax.ShapeDtypeStruct(info.shape, F32))
    return call(kernel, outs, [], own, info, *arrived, spare=after, time=1.0)


def finish_queries(own, late, side, near, along, info, devices, after):
    body, rows = own.shape

    def kernel(own_ref, info_ref, term_ref, *refs):
        s_refs, refs = refs[: len(side)], refs[len(side) :]
        a_refs, (loss_ref, out_ref) = refs[: len(along)], refs[-2:]
        bound = info_ref[3:4, :1]
        total = own_ref[...]
        for ref in s_refs[:late]:
            total = total + decoded(ref[:body, :], bound)
        for g in range(body // 128):
            here = slice(g * 128, (g + 1) * 128)
            out_ref[:, here] = 0.5 * total[here, :].T
        sides = [info_ref[1:2, :1]] + [read_term(ref) for ref in s_refs]
        lines = [info_ref[0:1, :1] + read_term(term_ref)] + [read_term(ref) for ref in a_refs]
        loss = tree(jnp.add, sides) + tree(jnp.add, lines)
        loss_ref[...] = loss * (1.0 / (2.0 * rows * devices))

    outs = (jax.ShapeDtypeStruct((1, 1), F32), jax.ShapeDtypeStruct((rows, body), F32))
    return call(kernel, outs, [], own, info, near, *side, *along, spare=[after], time=1.0)


def per_device(queries, passages, hard_ids, list_lengths):
    rows, width = queries.shape
    listed = hard_ids.shape[1]
    across = lax.axis_size("pa")
    down = lax.axis_size("pb")
    tall, wide = across * rows, down * rows

    message, near_message, far_message = first_messages(
        queries, passages, hard_ids, list_lengths
    )
    far = [exchange(far_message, "pb", j) for j in range(2, down, 2)]
    near = exchange(near_message, "pb", 1)
    passage_slots = [near_message, near]
    for part in far:
        passage_slots += [part, exchange(part, "pb", 1)]
    row_turns = list(range(0, across, 2))
    messages, counts = [], []
    for k in row_turns:
        part = exchange(message, "pa", k) if k else message
        part, count = count_listed(part, listed, down, [*far, counts[0], *([near] if k == across - 2 else [])] if k else [])
        other, other_count = count_listed(exchange(part, "pa", 1), listed, down)
        messages += [part, other]
        counts += [count, other_count]

    scores, stats, q_all, p_all = score_sweep(messages, passage_slots, counts, rows, width)
    passages = flipped(p_all)
    stats = share_out(stats, exchange(stats, "pa", 1), tall, wide, rows, passages)
    others = []
    for t in range(1, down):
        pairs = []
        for i in range(across * down):
            z, c = divmod(i, across)
            pairs.append((i, z * across + (c ^ 2 * t) if c % 2 == 0 else (z ^ t) * across + c))
        others.append(lax.ppermute(stats, ("pb", "pa"), pairs))
    stats = share_all(stats, others, rows)
    row_level, col_level, info = levels(stats, exchange(stats, "pa", 1), wide, rows)

    swept = (scores, row_level, col_level, counts)
    onward = list(range(3, down, 2))
    staying = [*range(2, down, 2), 1, 0]
    first = weight_sweep(onward, *swept)
    (near,) = passage_sweep(onward, onward, first, q_all, info, True)
    near = exchange(near, "pb", 1)
    second = weight_sweep(staying, *swept)
    weights = [*first, *second]
    blocks = passage_sweep(staying[:-2], staying, second, q_all, info)
    (last,) = passage_sweep([1], staying, second, q_all, info)
    last = exchange(last, "pb", 1)
    (passage_sum,) = passage_sweep([0], staying, second, q_all, info)

    side = []
    for m in range(across // 2):
        own, other = query_sweep([m], weights, [onward, staying], passages, info)
        other = exchange(other, "pa", 1)
        if m:
            after = [last] if m == 2 else []
            message = send_on(own, other, info, 3, 1, after=after)
            side.append(exchange(message, "pa", 2 * m))
        else:
            query_sum, core = own, other
    along = [
        exchange(send_on(own, near, info, 2, 0, part, 16, [message]), "pb", 2 * (part + 1))
        for part, own in enumerate(blocks)
    ]
    query_sum = added(query_sum, [(core, 0), (side[-1], 0)], info, 3)
    grad_passages, after = finish_passages(
        passage_sum, [last, *along], info, width, [query_sum]
    )
    loss, grad_queries = finish_queries(
        query_sum, len(side) - 1, side, near, along, info, across * down, after
    )
    return (loss.reshape(()), grad_queries, grad_passages)


def solution(mesh):
    return jax.shard_map(
        per_device,
        mesh=mesh,
        in_specs=(
            P(("pb", "pa"), None),
            P(("pb", "pa"), None),
            P(("pb", "pa"), None),
            P(("pb", "pa")),
        ),
        out_specs=(P(), P(("pb", "pa"), None), P(("pb", "pa"), None)),
        check_vma=False,
    )
```
